32 devices in a mesh: gx: 4 (over x, core), gy: 8 (over z, y).
Axes of the slice: x: 2, y: 2, z: 4, core: 2. Of those that a mesh axis runs over, the one named last changes fastest.
Arguments:
- fine_latent: bfloat16 [128, 1024, 256], P('gx', 'gy'), may hold values from -6 to 6
- nbr_dir: int32 [128, 6, 1024], P('gx', None, 'gy'), may hold values from 0 to 7
- nbr_mask: int32 [128, 6, 1024], P('gx', None, 'gy'), may hold values 0 or 1
- dir_embed: bfloat16 [8, 256], replicated, may hold values from -6 to 6
- w_center: bfloat16 [256, 256], replicated, may hold values from -0.375 to 0.375
- w_neighbour: bfloat16 [256, 256], replicated, may hold values from -0.375 to 0.375
- w_msg: bfloat16 [256, 256], replicated, may hold values from -0.375 to 0.375
- w_node_in: bfloat16 [512, 256], replicated, may hold values from -0.25 to 0.25
- w_node_out: bfloat16 [256, 256], replicated, may hold values from -0.375 to 0.375
- restrict_weight: bfloat16 [8, 128, 32, 128], P('gy', 'gx'), may hold values from -0.25 to 0.25
- cluster_host: int32 [8, 128, 1], P('gy', 'gx'), may hold values from 0 to 7; in each aligned block of 32 rows (0 to 31, 32 to 63, ..., all dimensions but the last counted through in order) at most 8 rows name the same one
- cluster_slot: int32 [8, 128], P('gy', 'gx'), may hold values from 0 to 7
- coarse_src: int32 [8192, 6], P(('gx', 'gy')), may hold values from 0 to 8191, as said below
- a_src: bfloat16 [256, 256], replicated, may hold values from -0.375 to 0.375
- a_dst: bfloat16 [256, 256], replicated, may hold values from -0.375 to 0.375
- a_msg: bfloat16 [256, 256], replicated, may hold values from -0.375 to 0.375
- b_in: bfloat16 [512, 256], replicated, may hold values from -0.25 to 0.25
- b_out: bfloat16 [256, 256], replicated, may hold values from -0.375 to 0.375
Outputs:
- fine_out: bfloat16 [128, 1024, 256], P('gx', 'gy')
The draws below stay inside these ranges and needn't reach their ends.
Inputs may be any that keep to these rules, and one draw needn't show every extreme that they name: `cluster_host`: among the 32 blocks of one device at most 8 name the same host; some device's blocks name one host exactly 8 times. coarse_src[n, j] lies in the strip of 2048 coarse rows that holds n, or in the next strip; rows of the last of the 4 strips take sources from their own strip only.
All inputs are finite; a program needn't handle non-finite values. No bound on the sum of `nbr_mask` on one device may be relied on, other than what follows from the above.
Results may differ from the reference program's by a relative error of at most 0.009.
Values may be sent and summed in bfloat16 or wider, within the bound.
No kernel may reach another device: no remote copies, remote signals or barrier semaphores. Data moves between devices by JAX's collectives and lax.ppermute only.
A program may use at most 64 MiB of HBM per device.

```python
import math
import jax
import jax.numpy as jnp
import numpy as np
from jax import lax

L = 256
CX = 32
CY = 128
K = 6
CR = 32
DEG_C = 6
CB_DEV = 8
CAP = 8
NX = 128
NY = 1024
NCLS = 64
STRIP = 2048
STRIPS = 4
NCOARSE = 8192
N_GY = 8


def draw_coarse_src(key, part):
    key = jax.random.fold_in(key, 11)
    first_key, second_key = jax.random.split(key)
    strip_index = jnp.arange(NCOARSE, dtype=jnp.int32) // STRIP
    stepped = jax.random.randint(first_key, (NCOARSE, DEG_C), 0, 2, dtype=jnp.int32)
    target = jnp.minimum(strip_index[:, None] + stepped, STRIPS - 1)
    within = jax.random.randint(second_key, (NCOARSE, DEG_C), 0, STRIP, dtype=jnp.int32)
    return (target * STRIP + within).astype(jnp.int32)


def place_ends(drawn, key, least, top_value):
    longest = drawn.shape.index(max(drawn.shape))
    spots = []
    for shift in (0, 1):
        where = [jax.random.randint(jax.random.fold_in(key, axis), (), 0, length) for axis, length in enumerate(drawn.shape)]
        where[longest] = (where[longest] + shift) % drawn.shape[longest]
        spots.append(tuple(where))
    return drawn.at[spots[0]].set(least).at[spots[1]].set(top_value)


def block_scale(stream_key, extent, cuts, least, high):
    loudness, own = 1.0, jax.random.fold_in(stream_key, 6)
    for axis_at, shards_of in cuts:
        steps = jnp.exp(jax.random.uniform(jax.random.fold_in(own, axis_at), (shards_of,), jnp.float32, least / len(cuts), high / len(cuts)))
        loudness = loudness * jnp.repeat(steps, extent[axis_at] // shards_of).reshape([-1 if axis == axis_at else 1 for axis in range(len(extent))])
    return loudness


def routed_block(stream_key, own, number, rows, count, top, limit, skew):
    order = jax.random.permutation(stream_key, count)
    crowded, common = load_shares(count, rows * top, limit, skew, True), load_shares(count, rows * top, limit, skew, False)
    places = jnp.arange(count)

    def named(lengths, offset_by):
        used = int((lengths > 0).sum())
        fixed = max(1, used // 4)
        moved = fixed + (places - fixed + offset_by * (used - fixed)) % max(1, count - fixed)
        return jnp.zeros((count,), jnp.int32).at[order[jnp.where(places < fixed, places, moved)]].set(jnp.asarray(lengths, jnp.int32))

    lengths = jnp.where(number % 4 == 0, named(crowded, number // 4), named(common, number - number // 4 - 1))
    mixed = jax.random.permutation(jax.random.fold_in(own, 3), count)
    donor, receiver = mixed[0:count // 2 * 2:2], mixed[1:count // 2 * 2:2]
    room = jnp.minimum(lengths[donor] - 1, limit - lengths[receiver]) // 2
    room = jnp.where((donor == order[0]) | (receiver == order[0]) | (lengths[receiver] == 0), 0, jnp.maximum(room, 0))
    moved = jax.random.randint(jax.random.fold_in(own, 4), (count // 2,), 0, 1 << 20) % (room + 1)
    lengths = lengths.at[donor].add(-moved).at[receiver].add(moved)
    labels = jnp.searchsorted(jnp.cumsum(lengths), jnp.arange(rows * top), side="right").astype(jnp.int32)
    table = labels.reshape(top, rows).T
    table = table[jax.random.permutation(jax.random.fold_in(own, 1), rows)]
    offset_by = jax.random.randint(jax.random.fold_in(own, 2), (rows, 1), 0, top)
    return jnp.take_along_axis(table, (jnp.arange(top)[None, :] + offset_by) % top, axis=1)


def load_shares(amount, total, reach, lean, full):
    weights = [(1 << 20) // math.isqrt(standing ** lean) + 1 for standing in range(1, amount + 1)]
    largest = reach if full else min(reach, max(-(-total // amount), total * weights[0] // sum(weights)))
    least = 1 if total - largest >= amount - 1 else 0
    given, rest = [largest] + [least] * (amount - 1), total - largest - least * (amount - 1)
    while rest > 0:
        candidates = [i for i in range(1, amount) if given[i] < largest] or [i for i in range(1, amount) if given[i] < reach]
        whole, budget = sum([weights[i] for i in candidates]), rest
        for i in candidates:
            extra = min(reach - given[i], max(1, budget * weights[i] // whole), rest)
            given[i] = given[i] + extra
            rest = rest - extra
    return np.array(given)


def noise(stream_key, extent, deviation, most, cuts=(), kind=jnp.bfloat16):
    result = jax.random.normal(stream_key, extent, jnp.float32) * deviation
    if len(cuts) > 0:
        result = block_scale(stream_key, extent, cuts, -0.22, 0.18) * result
    return jnp.clip(result, min=-most, max=most).astype(kind)


def setup_inputs(seed: int = 0) -> dict:
    key_of = jax.random.split(jax.random.key(seed), 19)
    fine_latent = noise(key_of[0], (NX, NY, L), 1.0, 6.0, ((0, 4), (1, 8)))
    nbr_dir = place_ends(jax.random.randint(key_of[1], (NX, K, NY), 0, 8), jax.random.fold_in(key_of[1], 1), 0, 7).astype(jnp.int32)
    nbr_mask = place_ends((jax.random.randint(key_of[2], (NX, K, NY), 0, 4) < 3).astype(jnp.int32), jax.random.fold_in(key_of[2], 1), 0, 1)
    dir_embed = noise(key_of[3], (8, L), 1.0, 6.0)
    w_center = noise(key_of[4], (L, L), L ** -0.5, 0.375)
    w_neighbour = noise(key_of[5], (L, L), L ** -0.5, 0.375)
    w_msg = noise(key_of[6], (L, L), L ** -0.5, 0.375)
    w_node_in = noise(key_of[7], (2 * L, L), (2 * L) ** -0.5, 0.25)
    w_node_out = noise(key_of[8], (L, L), L ** -0.5, 0.375)
    restrict_weight = noise(key_of[9], (N_GY, NX, CR, CY), (4 * CY) ** -0.5, 0.25, ((0, 8), (1, 4)))
    cluster_host_keys = jax.random.split(jax.random.fold_in(key_of[10], 1), N_GY * NX // CX)
    cluster_host_turns = jax.random.permutation(jax.random.fold_in(key_of[10], 3), N_GY * NX // CX)
    cluster_host = jax.vmap(lambda own, number: routed_block(jax.random.fold_in(key_of[10], 2), own, number, CX, N_GY, 1, CAP, 2))(cluster_host_keys, cluster_host_turns).reshape((N_GY, NX, 1))
    cluster_slot = place_ends(jax.random.randint(key_of[11], (N_GY, NX), 0, CB_DEV), jax.random.fold_in(key_of[11], 1), 0, CB_DEV - 1).astype(jnp.int32)
    coarse_src = draw_coarse_src(jax.random.fold_in(key_of[18], 71), 0)
    a_src = noise(key_of[13], (L, L), L ** -0.5, 0.375)
    a_dst = noise(key_of[14], (L, L), L ** -0.5, 0.375)
    a_msg = noise(key_of[15], (L, L), L ** -0.5, 0.375)
    b_in = noise(key_of[16], (2 * L, L), (2 * L) ** -0.5, 0.25)
    b_out = noise(key_of[17], (L, L), L ** -0.5, 0.375)
    return {"fine_latent": fine_latent, "nbr_dir": nbr_dir, "nbr_mask": nbr_mask, "dir_embed": dir_embed, "w_center": w_center, "w_neighbour": w_neighbour, "w_msg": w_msg, "w_node_in": w_node_in, "w_node_out": w_node_out, "restrict_weight": restrict_weight, "cluster_host": cluster_host, "cluster_slot": cluster_slot, "coarse_src": coarse_src, "a_src": a_src, "a_dst": a_dst, "a_msg": a_msg, "b_in": b_in, "b_out": b_out}


STEP_X = (-1, -1, -1, 0, 0, 1, 1, 1)
STEP_Y = (-1, 0, 1, -1, 1, -1, 0, 1)


def reference(fine_latent, nbr_dir, nbr_mask, dir_embed, w_center, w_neighbour, w_msg, w_node_in, w_node_out, restrict_weight, cluster_host, cluster_slot, coarse_src, a_src, a_dst, a_msg, b_in, b_out):
    grid_x, grid_y, feature_width = fine_latent.shape
    flattened = fine_latent.reshape(grid_x * grid_y, feature_width)
    center = jnp.dot(flattened, w_center, preferred_element_type=jnp.float32).reshape(grid_x, grid_y, feature_width)
    neighbour_proj = jnp.dot(flattened, w_neighbour, preferred_element_type=jnp.float32).astype(jnp.bfloat16)
    padded = jnp.pad(neighbour_proj.reshape(grid_x, grid_y, feature_width), ((1, 1), (1, 1), (0, 0)))
    table_x = jnp.array(STEP_X, dtype=jnp.int32)
    table_y = jnp.array(STEP_Y, dtype=jnp.int32)
    index_x = jnp.arange(grid_x, dtype=jnp.int32)[:, None]
    index_y = jnp.arange(grid_y, dtype=jnp.int32)[None, :]
    embedding = dir_embed.astype(jnp.float32)
    aggregate = jnp.zeros((grid_x, grid_y, feature_width), jnp.float32)
    for slot_index in range(K):
        direction = nbr_dir[:, slot_index, :]
        near_x = (index_x + 1 + table_x[direction]).astype(jnp.int32)
        near_y = (index_y + 1 + table_y[direction]).astype(jnp.int32)
        shifted = padded[near_x, near_y]
        hidden = jax.nn.relu(center + shifted.astype(jnp.float32) + embedding[direction]).astype(jnp.bfloat16)
        message = jnp.dot(hidden.reshape(-1, feature_width), w_msg, preferred_element_type=jnp.float32)
        weight_live = nbr_mask[:, slot_index, :].astype(jnp.float32)[:, :, None]
        aggregate = aggregate + weight_live * message.reshape(grid_x, grid_y, feature_width)
    joined = jnp.concatenate([flattened, aggregate.reshape(-1, feature_width).astype(jnp.bfloat16)], axis=1)
    node_hidden = jax.nn.relu(jnp.dot(joined, w_node_in, preferred_element_type=jnp.float32)).astype(jnp.bfloat16)
    refined = (flattened.astype(jnp.float32) + jnp.dot(node_hidden, w_node_out, preferred_element_type=jnp.float32)).astype(jnp.bfloat16)
    blocks = refined.reshape(grid_x, N_GY, CY, feature_width)
    weights = jnp.swapaxes(restrict_weight, 0, 1)
    restricted = jnp.einsum("xbrc,xbcl->xbrl", weights.astype(jnp.float32), blocks.astype(jnp.float32), precision=lax.Precision.HIGHEST)
    strip_index = (jnp.arange(grid_x, dtype=jnp.int32) // CX)[:, None]
    block_hosts = jnp.swapaxes(cluster_host[:, :, 0], 0, 1)
    block_slots = jnp.swapaxes(cluster_slot, 0, 1)
    cluster = (strip_index * NCLS + block_hosts * CB_DEV + block_slots).astype(jnp.int32)
    summed = jax.ops.segment_sum(restricted.reshape(grid_x * N_GY, CR * feature_width), cluster.reshape(-1), num_segments=STRIPS * NCLS)
    coarse_in = summed.reshape(NCOARSE, feature_width).astype(jnp.bfloat16)
    source_proj = jnp.dot(coarse_in, a_src, preferred_element_type=jnp.float32).astype(jnp.bfloat16)
    dest_proj = jnp.dot(coarse_in, a_dst, preferred_element_type=jnp.float32)
    gathered = source_proj[coarse_src]
    coarse_hidden = jax.nn.relu(gathered.astype(jnp.float32) + dest_proj[:, None, :]).astype(jnp.bfloat16)
    messages = jnp.dot(coarse_hidden.reshape(-1, feature_width), a_msg, preferred_element_type=jnp.float32)
    coarse_aggregate = jnp.sum(messages.reshape(NCOARSE, DEG_C, feature_width), axis=1).astype(jnp.bfloat16)
    coarse_joined = jnp.concatenate([coarse_in, coarse_aggregate], axis=1)
    coarse_node = jax.nn.relu(jnp.dot(coarse_joined, b_in, preferred_element_type=jnp.float32)).astype(jnp.bfloat16)
    coarse_out = (coarse_in.astype(jnp.float32) + jnp.dot(coarse_node, b_out, preferred_element_type=jnp.float32)).astype(jnp.bfloat16)
    picked = coarse_out.reshape(STRIPS * NCLS, CR, feature_width)[cluster]
    prolonged = jnp.einsum("xbrc,xbrl->xbcl", weights.astype(jnp.float32), picked.astype(jnp.float32), precision=lax.Precision.HIGHEST)
    fine_out = (blocks.astype(jnp.float32) + prolonged).astype(jnp.bfloat16)
    return fine_out.reshape(grid_x, grid_y, feature_width)
```

```python
import functools

import jax
import jax.numpy as jnp
from jax import lax
from jax.experimental import pallas as pl
from jax.experimental.pallas import tpu as pltpu
from jax.sharding import PartitionSpec as P

STEP_X = (-1, -1, -1, 0, 0, 1, 1, 1)
STEP_Y = (-1, 0, 1, -1, 1, -1, 0, 1)
F32 = jnp.float32
BF16 = jnp.bfloat16
VMEM_LIMIT = 56 << 20


def dot(a, b):
    return jnp.dot(a, b, preferred_element_type=F32)


def fine_kernel(
    hosts,
    rows_per_chunk,
    offset_ref,
    latent_ref,
    ends_ref,
    sides_ref,
    counts_ref,
    embed_ref,
    wc_ref,
    wn_ref,
    wm_ref,
    wi_ref,
    wo_ref,
    weight_ref,
    refined_ref,
    *rest,
):
    partial_refs = rest[:hosts]
    proj_ref, center_ref, summed_ref, side_ref, total_ref = rest[hosts:]
    cells_x, cells_y, width = latent_ref.shape
    total_ref[...] = jnp.zeros_like(total_ref)
    place = lax.broadcasted_iota(jnp.int32, (cells_y, width), 0)

    padded = sides_ref.shape[1]
    side_ref[0] = dot(sides_ref[0], wn_ref[...]).astype(BF16).astype(F32)
    side_ref[1] = dot(sides_ref[1], wn_ref[...]).astype(BF16).astype(F32)

    def store_row(row, proj):
        low = side_ref[0, pl.ds(row, 1), :]
        high = side_ref[1, pl.ds(row, 1), :]
        proj_ref[1, row] = proj
        proj_ref[0, row] = jnp.where(place == 0, low, pltpu.roll(proj, 1, 0))
        proj_ref[2, row] = jnp.where(
            place == cells_y - 1, high, pltpu.roll(proj, cells_y - 1, 0)
        )

    for end, row in ((0, 0), (1, cells_x + 1)):
        store_row(row, dot(ends_ref[end], wn_ref[...]).astype(BF16).astype(F32))

    def project(chunk, carry):
        first = chunk * rows_per_chunk
        cells = latent_ref[pl.ds(first, rows_per_chunk)].reshape(-1, width)
        proj = dot(cells, wn_ref[...]).astype(BF16).astype(F32)
        for row in range(rows_per_chunk):
            store_row(first + row + 1, proj[row * cells_y : (row + 1) * cells_y])
        return carry

    lax.fori_loop(0, cells_x // rows_per_chunk, project, 0)

    tile = 32

    def refine(chunk, carry):
        first = chunk * rows_per_chunk
        cells = latent_ref[pl.ds(first, rows_per_chunk)].reshape(-1, width)
        center_ref[...] = dot(cells, wc_ref[...]).reshape(rows_per_chunk, cells_y, width)

        def gather(row, inner):
            x = first + row
            live = counts_ref[x].T
            for start in range(0, cells_y, tile):
                span = slice(start, start + tile)
                center = center_ref[row, span, :]
                total = None
                for d in range(8):
                    near = proj_ref[1 + STEP_Y[d], x + 1 + STEP_X[d], span, :]
                    hidden = jnp.maximum(center + near + embed_ref[d : d + 1, :], 0.0)
                    term = live[span, d : d + 1] * hidden
                    total = term if total is None else total + term
                summed_ref[row, span, :] = total.astype(BF16)
            return inner

        lax.fori_loop(0, rows_per_chunk, gather, 0)
        aggregate = dot(summed_ref[...].reshape(-1, width), wm_ref[...]).astype(BF16)
        hidden = dot(cells, wi_ref[:width]) + dot(aggregate, wi_ref[width:])
        hidden = jnp.maximum(hidden, 0.0).astype(BF16)
        refined = (cells.astype(F32) + dot(hidden, wo_ref[...])).astype(BF16)
        refined_ref[pl.ds(first, rows_per_chunk)] = refined.reshape(
            rows_per_chunk, cells_y, width
        )
        for row in range(rows_per_chunk):
            x = first + row
            block = refined[row * cells_y : (row + 1) * cells_y]
            rows = weight_ref.shape[1]
            part = dot(weight_ref[x], block)
            base = pl.multiple_of(offset_ref[x], rows)
            total_ref[pl.ds(base, rows), :] += part
        return carry

    lax.fori_loop(0, cells_x // rows_per_chunk, refine, 0)
    size = partial_refs[0].shape[0]
    for host in range(hosts):
        partial_refs[host][...] = total_ref[host * size : (host + 1) * size, :].astype(BF16)


def coarse_kernel(
    hosts,
    place_ref,
    source_ref,
    edge_ref,
    refined_ref,
    weight_ref,
    as_ref,
    ad_ref,
    am_ref,
    bi_ref,
    bo_ref,
    *rest,
):
    own_refs = rest[:hosts]
    next_refs = rest[hosts : 2 * hosts]
    out_ref, strip_ref, table_ref, rows_ref, dest_ref, summed_ref = rest[2 * hosts :]
    blocks, rows, _ = weight_ref.shape
    size, width = own_refs[0].shape
    half = width // 2
    degree = source_ref.shape[0] // (hosts * size)

    def split_store(ref, first, value):
        count = value.shape[0]
        ref[pl.ds(2 * first, count, stride=2), :] = value[:, :half]
        ref[pl.ds(2 * first + 1, count, stride=2), :] = value[:, half:]

    for number, ref in enumerate(own_refs + next_refs):
        proj = dot(ref[...], as_ref[...]).astype(BF16).astype(F32)
        split_store(table_ref, number * size, proj)
    for number, ref in enumerate(own_refs):
        strip_ref[pl.ds(number * size, size), :] = ref[...]

    def pick(block, carry):
        base = pl.multiple_of(place_ref[block], rows)
        rows_ref[pl.ds(pl.multiple_of(block * rows, rows), rows), :] = strip_ref[
            pl.ds(base, rows), :
        ]
        return carry

    lax.fori_loop(0, blocks, pick, 0)
    for first in range(0, blocks * rows, 256):
        split_store(dest_ref, first, dot(rows_ref[first : first + 256, :], ad_ref[...]))

    def gather(block, carry):
        edge = edge_ref[block]
        for row in range(rows):
            at = pl.ds(pl.multiple_of(2 * (block * rows + row), 2), 2)
            dest = dest_ref[at, :]
            total = None
            for slot in range(degree):
                source = source_ref[edge + row * degree + slot]
                near = table_ref[pl.ds(pl.multiple_of(2 * source, 2), 2), :]
                hidden = jnp.maximum(near + dest, 0.0)
                total = hidden if total is None else total + hidden
            summed_ref[at, :] = total
        return carry

    lax.fori_loop(0, blocks, gather, 0)
    step = 8

    def update(group, carry):
        first = pl.multiple_of(group * step * rows, step * rows)
        base = rows_ref[pl.ds(first, step * rows), :]
        summed = jnp.concatenate(
            [summed_ref[pl.ds(2 * first + part, step * rows, stride=2), :] for part in (0, 1)],
            axis=1,
        ).astype(BF16)
        aggregate = dot(summed, am_ref[...]).astype(BF16)
        hidden = dot(base, bi_ref[:width]) + dot(aggregate, bi_ref[width:])
        hidden = jnp.maximum(hidden, 0.0).astype(BF16)
        result = (base.astype(F32) + dot(hidden, bo_ref[...])).astype(BF16)
        for part in range(step):
            block = group * step + part
            raised = lax.dot_general(
                weight_ref[block],
                result[part * rows : (part + 1) * rows],
                (((0,), (0,)), ((), ())),
                preferred_element_type=F32,
            )
            out_ref[block] = (refined_ref[block].astype(F32) + raised).astype(BF16)
        return carry

    lax.fori_loop(0, blocks // step, update, 0)


def shifted(value, axis, step):
    count = lax.axis_size(axis)
    pairs = [(i, i + step) for i in range(count) if 0 <= i + step < count]
    return lax.ppermute(value, axis, pairs)


def swapped(value, axis, distance):
    count = lax.axis_size(axis)
    return lax.ppermute(value, axis, [(i, i ^ distance) for i in range(count)])


def per_device(
    fine_latent,
    nbr_dir,
    nbr_mask,
    dir_embed,
    w_center,
    w_neighbour,
    w_msg,
    w_node_in,
    w_node_out,
    restrict_weight,
    cluster_host,
    cluster_slot,
    coarse_src,
    a_src,
    a_dst,
    a_msg,
    b_in,
    b_out,
):
    cells_x, cells_y, width = fine_latent.shape
    hosts = lax.axis_size("gy")
    outer = 4
    inner = hosts // outer
    me = lax.axis_index("gy")
    weights = restrict_weight[0]
    blocks, rows, _ = weights.shape
    per_host = blocks // 4
    size = per_host * rows
    degree = coarse_src.shape[1]

    strip_src = lax.all_gather(coarse_src.reshape(-1), "gy", axis=0, tiled=True)

    low = shifted(fine_latent[:, -1, :], "gy", 1)
    high = shifted(fine_latent[:, 0, :], "gy", -1)
    first_row = jnp.concatenate([fine_latent[0], low[:1], high[:1]], axis=0)
    last_row = jnp.concatenate([fine_latent[-1], low[-1:], high[-1:]], axis=0)
    above = shifted(last_row, "gx", 1)
    below = shifted(first_row, "gx", -1)
    ends = jnp.stack([above[:cells_y], below[:cells_y]])
    extra = -(cells_x + 2) % 16
    fill = jnp.zeros((extra, width), BF16)
    sides = jnp.stack(
        [
            jnp.concatenate([above[cells_y : cells_y + 1], low, below[cells_y : cells_y + 1], fill]),
            jnp.concatenate([above[cells_y + 1 :], high, below[cells_y + 1 :], fill]),
        ]
    )
    padded = cells_x + 2 + extra

    live = nbr_mask.astype(F32)
    counts = jnp.stack(
        [jnp.sum(jnp.where(nbr_dir == d, live, 0.0), axis=1) for d in range(8)], axis=1
    )

    relative = cluster_host[0, :, 0] ^ me
    offsets = (relative * per_host + cluster_slot[0]) * rows
    edges = (cluster_host[0, :, 0] * per_host + cluster_slot[0]) * (rows * degree)

    vmem = pl.BlockSpec(memory_space=pltpu.VMEM)
    smem = pl.BlockSpec(memory_space=pltpu.SMEM)
    chunk = 8
    fine = pl.pallas_call(
        functools.partial(fine_kernel, hosts, chunk),
        out_shape=[jax.ShapeDtypeStruct(fine_latent.shape, BF16)]
        + [jax.ShapeDtypeStruct((size, width), BF16)] * hosts,
        in_specs=[smem] + [vmem] * 11,
        out_specs=[vmem] * (1 + hosts),
        scratch_shapes=[
            pltpu.VMEM((3, cells_x + 2, cells_y, width), F32),
            pltpu.VMEM((chunk, cells_y, width), F32),
            pltpu.VMEM((chunk, cells_y, width), BF16),
            pltpu.VMEM((2, padded, width), F32),
            pltpu.VMEM((hosts * size, width), F32),
        ],
        compiler_params=pltpu.CompilerParams(vmem_limit_bytes=VMEM_LIMIT),
        name="fine_cells",
    )(
        offsets,
        fine_latent,
        ends,
        sides,
        counts,
        dir_embed.astype(F32),
        w_center,
        w_neighbour,
        w_msg,
        w_node_in,
        w_node_out,
        weights,
    )
    refined, partial = fine[0], fine[1:]

    parts = {}
    for far in reversed(range(outer)):
        total = partial[far * inner].astype(F32)
        for near in range(1, inner):
            total = total + swapped(partial[far * inner + near], "gy", near).astype(F32)
        parts[far] = total
    coarse_in = parts[0]
    for far in reversed(range(1, outer)):
        coarse_in = coarse_in + swapped(parts[far].astype(BF16), "gy", far * inner).astype(F32)
    coarse_in = coarse_in.astype(BF16)

    own = [None] * hosts
    own[0] = coarse_in
    for far in range(1, outer):
        own[far * inner] = swapped(coarse_in, "gy", far * inner)
    for far in range(outer):
        for near in range(1, inner):
            own[far * inner + near] = swapped(own[far * inner], "gy", near)
    following = [shifted(value, "gx", -1) for value in own]

    strip_rows = hosts * size
    local = strip_src - lax.axis_index("gx") * strip_rows
    local = jnp.clip(local, 0, 2 * strip_rows - 1) ^ (me * size)

    return pl.pallas_call(
        functools.partial(coarse_kernel, hosts),
        out_shape=jax.ShapeDtypeStruct(fine_latent.shape, BF16),
        in_specs=[smem] * 3 + [vmem] * (7 + 2 * hosts),
        out_specs=vmem,
        scratch_shapes=[
            pltpu.VMEM((strip_rows, width), BF16),
            pltpu.VMEM((4 * strip_rows, width // 2), F32),
            pltpu.VMEM((blocks * rows, width), BF16),
            pltpu.VMEM((2 * blocks * rows, width // 2), F32),
            pltpu.VMEM((2 * blocks * rows, width // 2), F32),
        ],
        compiler_params=pltpu.CompilerParams(vmem_limit_bytes=VMEM_LIMIT),
        name="coarse_rows",
    )(offsets, local, edges, refined, weights, a_src, a_dst, a_msg, b_in, b_out, *own, *following)


def solution(mesh):
    in_specs = (
        P("gx", "gy", None),
        P("gx", None, "gy"),
        P("gx", None, "gy"),
        P(),
        P(),
        P(),
        P(),
        P(),
        P(),
        P("gy", "gx", None, None),
        P("gy", "gx", None),
        P("gy", "gx"),
        P(("gx", "gy"), None),
        P(),
        P(),
        P(),
        P(),
        P(),
    )
    out_specs = P("gx", "gy", None)
    return jax.shard_map(
        per_device, mesh=mesh, in_specs=in_specs, out_specs=out_specs, check_vma=False
    )
```

```python
import functools

import jax
import jax.numpy as jnp
from jax import lax
from jax.experimental import pallas as pl
from jax.experimental.pallas import tpu as pltpu
from jax.sharding import PartitionSpec as P

STEP_X = (-1, -1, -1, 0, 0, 1, 1, 1)
STEP_Y = (-1, 0, 1, -1, 1, -1, 0, 1)
F32 = jnp.float32
BF16 = jnp.bfloat16
DIGIT = 128
VMEM_LIMIT = 56 << 20


def dot(a, b):
    return jnp.dot(a, b, preferred_element_type=F32)


def fine_kernel(
    hosts,
    rows_per_chunk,
    host_ref,
    slot_ref,
    latent_ref,
    low_ref,
    high_ref,
    above_ref,
    below_ref,
    dir_ref,
    mask_ref,
    embed_ref,
    wc_ref,
    wn_ref,
    wm_ref,
    wi_ref,
    wo_ref,
    weight_ref,
    refined_ref,
    *rest,
):
    partial_refs = rest[:hosts]
    proj_ref, center_ref, summed_ref, side_ref, total_ref, count_ref, spread_ref = rest[hosts : hosts + 7]
    cells_ref, result_ref, load_sem, save_sem = rest[hosts + 7 :]
    cells_x, cells_y, width = latent_ref.shape
    me, strip = lax.axis_index("gy"), lax.axis_index("gx")
    flags = (me > 0, me < hosts - 1, strip > 0, strip < lax.axis_size("gx") - 1)
    chunks = cells_x // rows_per_chunk

    def load(chunk):
        part = pl.ds(chunk * rows_per_chunk, rows_per_chunk)
        return pltpu.make_async_copy(latent_ref.at[part], cells_ref.at[part], load_sem.at[chunk])

    def save(chunk):
        part = pl.ds(chunk * rows_per_chunk, rows_per_chunk)
        return pltpu.make_async_copy(result_ref.at[part], refined_ref.at[part], save_sem.at[chunk])

    for chunk in range(chunks):
        load(chunk).start()
    lanes = 128
    size = partial_refs[0].shape[0]
    total_ref[...] = jnp.zeros_like(total_ref)
    place = lax.broadcasted_iota(jnp.int32, (cells_y, width), 0)

    def project(cells):
        return dot(cells, wn_ref[...]).astype(BF16).astype(F32)

    def present(number, proj):
        return jnp.where(flags[number], proj, 0.0)

    def store_row(row, proj):
        low = side_ref[0, pl.ds(row, 1), :]
        high = side_ref[1, pl.ds(row, 1), :]
        proj_ref[1, row] = proj
        proj_ref[0, row] = jnp.where(place == 0, low, pltpu.roll(proj, 1, 0))
        proj_ref[2, row] = jnp.where(
            place == cells_y - 1, high, pltpu.roll(proj, cells_y - 1, 0)
        )

    side_ref[0, 1 : cells_x + 1, :] = present(0, project(low_ref[...]))
    side_ref[1, 1 : cells_x + 1, :] = present(1, project(high_ref[...]))
    for ref, number, row in ((above_ref, 2, 0), (below_ref, 3, cells_x + 1)):
        proj = present(number, project(ref[...]))
        for side in (0, 1):
            corner = proj[cells_y + side : cells_y + side + 1]
            side_ref[side, row : row + 1, :] = present(side, corner)
        store_row(row, proj[:cells_y])

    def prepare(chunk, carry):
        first = chunk * rows_per_chunk
        load(chunk).wait()
        proj = project(cells_ref[pl.ds(first, rows_per_chunk)].reshape(-1, width))
        for row in range(rows_per_chunk):
            store_row(first + row + 1, proj[row * cells_y : (row + 1) * cells_y])
        return carry

    lax.fori_loop(0, chunks, prepare, 0)
    for d in range(8):
        count = None
        for slot in range(dir_ref.shape[0]):
            term = jnp.where(dir_ref[slot] == d, mask_ref[slot].astype(F32), 0.0)
            count = term if count is None else count + term
        count_ref[pl.ds(d, cells_x, stride=8), :] = count

    lowest = -embed_ref[...].astype(F32)
    shape = (8, 8 * lanes)
    own_lanes = lax.broadcasted_iota(jnp.int32, shape, 1) // lanes
    ones = (own_lanes == lax.broadcasted_iota(jnp.int32, shape, 0)).astype(BF16)

    def columns(x, rows):
        count = count_ref[pl.ds(pl.multiple_of(x * 8, 8), 8), :]
        return lax.dot_general(
            count.astype(BF16), rows, (((0,), (0,)), ((), ())), preferred_element_type=F32
        )

    def refine(chunk, carry):
        first = chunk * rows_per_chunk
        cells = cells_ref[pl.ds(first, rows_per_chunk)].reshape(-1, width)
        center_ref[...] = dot(cells, wc_ref[...]).reshape(rows_per_chunk, cells_y, width)
        for row in range(rows_per_chunk):
            spread_ref[row] = columns(first + row, ones)

        def gather(row, inner):
            x = first + row
            for start in range(0, cells_y, 16):
                span = slice(start, start + 16)
                for half in range(0, width, lanes):
                    part = slice(half, half + lanes)
                    center = center_ref[row, span, part]
                    total = None
                    for d in range(8):
                        near = proj_ref[1 + STEP_Y[d], x + 1 + STEP_X[d], span, part]
                        hidden = jnp.maximum(center + near, lowest[d : d + 1, part])
                        term = spread_ref[row, span, d * lanes : (d + 1) * lanes] * hidden
                        total = term if total is None else total + term
                    summed_ref[row, span, part] = total
            return inner

        lax.fori_loop(0, rows_per_chunk, gather, 0)
        rest_sum = jnp.concatenate(
            [columns(first + row, embed_ref[...]) for row in range(rows_per_chunk)]
        )
        summed = (summed_ref[...].reshape(-1, width) + rest_sum).astype(BF16)
        aggregate = dot(summed, wm_ref[...]).astype(BF16)
        hidden = dot(cells, wi_ref[:width]) + dot(aggregate, wi_ref[width:])
        hidden = jnp.maximum(hidden, 0.0).astype(BF16)
        refined = (cells.astype(F32) + dot(hidden, wo_ref[...])).astype(BF16)
        result_ref[pl.ds(first, rows_per_chunk)] = refined.reshape(
            rows_per_chunk, cells_y, width
        )
        save(chunk).start()
        for row in range(rows_per_chunk):
            x = first + row
            rows = weight_ref.shape[1]
            part = dot(weight_ref[x], refined[row * cells_y : (row + 1) * cells_y])
            cluster = (host_ref[x] ^ me) * (size // rows) + slot_ref[x]
            base = pl.multiple_of(cluster * rows, rows)
            total_ref[pl.ds(base, rows), :] += part
        return carry

    lax.fori_loop(0, chunks, refine, 0)
    for host in range(hosts):
        partial_refs[host][...] = total_ref[host * size : (host + 1) * size, :].astype(BF16)
    for chunk in range(chunks):
        save(chunk).wait()


def coarse_kernel(
    hosts,
    degree,
    host_ref,
    slot_ref,
    refined_ref,
    weight_ref,
    as_ref,
    ad_ref,
    am_ref,
    bi_ref,
    bo_ref,
    *rest,
):
    own_refs = rest[:hosts]
    next_refs = rest[hosts : 2 * hosts]
    out_ref, strip_ref, table_ref, rows_ref, dest_ref, summed_ref = rest[2 * hosts : 2 * hosts + 6]
    cells_ref, result_ref, index_ref, lined_ref, source_ref, load_sem, save_sem, index_sem = rest[2 * hosts + 6 :]
    blocks, rows, _ = weight_ref.shape
    size, width = strip_ref.shape[0] // hosts, strip_ref.shape[1]
    lanes = 128
    me = lax.axis_index("gy")
    load = pltpu.make_async_copy(refined_ref, cells_ref, load_sem)
    load.start()

    def cluster_row(block):
        return ((host_ref[block] ^ me) * (size // rows) + slot_ref[block]) * rows

    half = width // 2
    for number, ref in enumerate(own_refs):
        digits = ref[size:, :].astype(F32).astype(jnp.int32)
        local = digits[:degree] * DIGIT + digits[degree : 2 * degree]
        local = 2 * (jnp.clip(local, 0, 2 * hosts * size - 1) ^ (me * size))
        for part in range(size // lanes):
            at = 8 * (number * (size // lanes) + part)
            index_ref[at : at + degree, :] = local[:, part * lanes : (part + 1) * lanes]

    def line_up(block, carry):
        first = cluster_row(block)
        line = pl.multiple_of(8 * (first // lanes), 8)
        turned_by = (lanes - first % lanes) % lanes
        at = pl.ds(pl.multiple_of(8 * block, 8), 8)
        lined_ref[at, :] = pltpu.roll(index_ref[pl.ds(line, 8), :], turned_by, 1)
        return carry

    lax.fori_loop(0, blocks, line_up, 0)
    index_copy = pltpu.make_async_copy(lined_ref, source_ref, index_sem)
    index_copy.start()

    def split_store(ref, first, value):
        count = value.shape[0]
        ref[pl.ds(2 * first, count, stride=2), :] = value[:, :half]
        ref[pl.ds(2 * first + 1, count, stride=2), :] = value[:, half:]

    for number, ref in enumerate(own_refs + next_refs):
        proj = dot(ref[:size, :], as_ref[...]).astype(BF16).astype(F32)
        split_store(table_ref, number * size, proj)
    for number, ref in enumerate(own_refs):
        strip_ref[pl.ds(number * size, size), :] = ref[:size, :]

    def pick(block, carry):
        base = pl.multiple_of(cluster_row(block), rows)
        rows_ref[pl.ds(pl.multiple_of(block * rows, rows), rows), :] = strip_ref[
            pl.ds(base, rows), :
        ]
        return carry

    lax.fori_loop(0, blocks, pick, 0)
    for first in range(0, blocks * rows, 256):
        split_store(dest_ref, first, dot(rows_ref[first : first + 256, :], ad_ref[...]))

    index_copy.wait()

    def gather(block, carry):
        line = 8 * block
        for row in range(rows):
            at = pl.ds(pl.multiple_of(2 * (block * rows + row), 2), 2)
            dest = dest_ref[at, :]
            total = None
            for slot in range(degree):
                source = source_ref[line + slot, row]
                near = table_ref[pl.ds(pl.multiple_of(source, 2), 2), :]
                hidden = jnp.maximum(near + dest, 0.0)
                total = hidden if total is None else total + hidden
            summed_ref[at, :] = total
        return carry

    lax.fori_loop(0, blocks, gather, 0)
    step = 8
    load.wait()

    def save(group):
        part = pl.ds(group * step, step)
        return pltpu.make_async_copy(result_ref.at[part], out_ref.at[part], save_sem.at[group])

    def update(group, carry):
        first = pl.multiple_of(group * step * rows, step * rows)
        base = rows_ref[pl.ds(first, step * rows), :]
        summed = jnp.concatenate(
            [summed_ref[pl.ds(2 * first + part, step * rows, stride=2), :] for part in (0, 1)],
            axis=1,
        ).astype(BF16)
        aggregate = dot(summed, am_ref[...]).astype(BF16)
        hidden = dot(base, bi_ref[:width]) + dot(aggregate, bi_ref[width:])
        hidden = jnp.maximum(hidden, 0.0).astype(BF16)
        result = (base.astype(F32) + dot(hidden, bo_ref[...])).astype(BF16)
        for part in range(step):
            block = group * step + part
            raised = lax.dot_general(
                weight_ref[block],
                result[part * rows : (part + 1) * rows],
                (((0,), (0,)), ((), ())),
                preferred_element_type=F32,
            )
            result_ref[block] = (cells_ref[block].astype(F32) + raised).astype(BF16)
        save(group).start()
        return carry

    lax.fori_loop(0, blocks // step, update, 0)
    for group in range(blocks // step):
        save(group).wait()


def turned(value, axis, step):
    count = lax.axis_size(axis)
    return lax.ppermute(value, axis, [(i, (i + step) % count) for i in range(count)])


def swapped(value, axis, distance):
    count = lax.axis_size(axis)
    return lax.ppermute(value, axis, [(i, i ^ distance) for i in range(count)])


def per_device(
    fine_latent,
    nbr_dir,
    nbr_mask,
    dir_embed,
    w_center,
    w_neighbour,
    w_msg,
    w_node_in,
    w_node_out,
    restrict_weight,
    cluster_host,
    cluster_slot,
    coarse_src,
    a_src,
    a_dst,
    a_msg,
    b_in,
    b_out,
):
    cells_x, cells_y, width = fine_latent.shape
    hosts = lax.axis_size("gy")
    outer = 4
    inner = hosts // outer
    me = lax.axis_index("gy")
    weights = restrict_weight[0]
    blocks, rows, _ = weights.shape
    per_host = blocks // 4
    size = per_host * rows
    degree = coarse_src.shape[1]

    low = turned(fine_latent[:, -1, :], "gy", 1)
    high = turned(fine_latent[:, 0, :], "gy", -1)
    fill = jnp.zeros((14, width), BF16)
    above = turned(jnp.concatenate([fine_latent[-1], low[-1:], high[-1:], fill]), "gx", 1)
    below = turned(jnp.concatenate([fine_latent[0], low[:1], high[:1], fill]), "gx", -1)
    vmem = pl.BlockSpec(memory_space=pltpu.VMEM)
    smem = pl.BlockSpec(memory_space=pltpu.SMEM)
    hbm = pl.BlockSpec(memory_space=pl.ANY)
    block_host, block_slot = cluster_host[0, :, 0], cluster_slot[0]
    chunk = 16
    fine = pl.pallas_call(
        functools.partial(fine_kernel, hosts, chunk),
        out_shape=[jax.ShapeDtypeStruct(fine_latent.shape, BF16)]
        + [jax.ShapeDtypeStruct((size, width), BF16)] * hosts,
        in_specs=[smem] * 2 + [hbm] + [vmem] * 13,
        out_specs=[hbm] + [vmem] * hosts,
        scratch_shapes=[
            pltpu.VMEM((3, cells_x + 2, cells_y, width), F32),
            pltpu.VMEM((chunk, cells_y, width), F32),
            pltpu.VMEM((chunk, cells_y, width), F32),
            pltpu.VMEM((2, cells_x + 8, width), F32),
            pltpu.VMEM((hosts * size, width), F32),
            pltpu.VMEM((cells_x * 8, cells_y), F32),
            pltpu.VMEM((chunk, cells_y, 8 * 128), F32),
            pltpu.VMEM(fine_latent.shape, BF16),
            pltpu.VMEM(fine_latent.shape, BF16),
            pltpu.SemaphoreType.DMA((cells_x // chunk,)),
            pltpu.SemaphoreType.DMA((cells_x // chunk,)),
        ],
        compiler_params=pltpu.CompilerParams(vmem_limit_bytes=VMEM_LIMIT),
        name="fine_cells",
    )(
        block_host,
        block_slot,
        fine_latent,
        low,
        high,
        above,
        below,
        jnp.swapaxes(nbr_dir, 0, 1),
        jnp.swapaxes(nbr_mask, 0, 1),
        dir_embed,
        w_center,
        w_neighbour,
        w_msg,
        w_node_in,
        w_node_out,
        weights,
    )
    refined, partial = fine[0], fine[1:]

    parts = {}
    for far in reversed(range(outer)):
        total = partial[far * inner].astype(F32)
        for near in range(1, inner):
            total = total + swapped(partial[far * inner + near], "gy", near).astype(F32)
        parts[far] = total
    coarse_in = parts[0]
    for far in reversed(range(1, outer)):
        coarse_in = coarse_in + swapped(parts[far].astype(BF16), "gy", far * inner).astype(F32)
    strip_rows = hosts * size
    local = coarse_src.T - lax.axis_index("gx") * strip_rows
    digits = [(local // DIGIT).astype(BF16), (local % DIGIT).astype(BF16)]
    digits = jnp.concatenate(digits + [jnp.zeros((16 - 2 * degree, size), BF16)])
    coarse_in = jnp.concatenate([coarse_in.astype(BF16), digits])

    own = [None] * hosts
    own[0] = coarse_in
    far = outer // 2
    own[far * inner] = swapped(coarse_in, "gy", far * inner)
    for step in range(1, far):
        own[step * inner] = swapped(coarse_in, "gy", step * inner)
        own[(far + step) * inner] = swapped(own[far * inner], "gy", step * inner)
    for far in range(outer):
        for near in range(1, inner):
            own[far * inner + near] = swapped(own[far * inner], "gy", near)
    following = [turned(value, "gx", -1) for value in own]

    return pl.pallas_call(
        functools.partial(coarse_kernel, hosts, degree),
        out_shape=jax.ShapeDtypeStruct(fine_latent.shape, BF16),
        in_specs=[smem] * 2 + [hbm] + [vmem] * (6 + 2 * hosts),
        out_specs=hbm,
        scratch_shapes=[
            pltpu.VMEM((strip_rows, width), BF16),
            pltpu.VMEM((4 * strip_rows, width // 2), F32),
            pltpu.VMEM((blocks * rows, width), BF16),
            pltpu.VMEM((2 * blocks * rows, width // 2), F32),
            pltpu.VMEM((2 * blocks * rows, width // 2), F32),
            pltpu.VMEM(fine_latent.shape, BF16),
            pltpu.VMEM(fine_latent.shape, BF16),
            pltpu.VMEM((8 * strip_rows // 128, 128), jnp.int32),
            pltpu.VMEM((8 * blocks, 128), jnp.int32),
            pltpu.SMEM((8 * blocks, 128), jnp.int32),
            pltpu.SemaphoreType.DMA(()),
            pltpu.SemaphoreType.DMA((4,)),
            pltpu.SemaphoreType.DMA(()),
        ],
        compiler_params=pltpu.CompilerParams(vmem_limit_bytes=VMEM_LIMIT),
        name="coarse_rows",
    )(block_host, block_slot, refined, weights, a_src, a_dst, a_msg, b_in, b_out, *own, *following)


def solution(mesh):
    in_specs = (
        P("gx", "gy", None),
        P("gx", None, "gy"),
        P("gx", None, "gy"),
        P(),
        P(),
        P(),
        P(),
        P(),
        P(),
        P("gy", "gx", None, None),
        P("gy", "gx", None),
        P("gy", "gx"),
        P(("gx", "gy"), None),
        P(),
        P(),
        P(),
        P(),
        P(),
    )
    out_specs = P("gx", "gy", None)
    return jax.shard_map(
        per_device, mesh=mesh, in_specs=in_specs, out_specs=out_specs, check_vma=False
    )
```

```python
import functools

import jax
import jax.numpy as jnp
from jax import lax
from jax.experimental import pallas as pl
from jax.experimental.pallas import tpu as pltpu
from jax.sharding import PartitionSpec as P

STEP_X = (-1, -1, -1, 0, 0, 1, 1, 1)
STEP_Y = (-1, 0, 1, -1, 1, -1, 0, 1)
F32 = jnp.float32
BF16 = jnp.bfloat16
DIGIT = 128
VMEM_LIMIT = 56 << 20


def dot(a, b):
    return jnp.dot(a, b, preferred_element_type=F32)


def fine_kernel(
    hosts,
    rows_per_chunk,
    host_ref,
    slot_ref,
    latent_ref,
    low_hbm,
    high_hbm,
    above_hbm,
    below_hbm,
    wc_hbm,
    wm_hbm,
    wi_hbm,
    wo_hbm,
    weight_hbm,
    dir_ref,
    mask_ref,
    embed_ref,
    wn_ref,
    refined_ref,
    *rest,
):
    partial_hbm = rest[:hosts]
    proj_ref, center_ref, summed_ref, side_ref, total_ref, count_ref, spread_ref = rest[hosts : hosts + 7]
    cells_ref, result_ref, partial_ref = rest[hosts + 7 : hosts + 10]
    low_ref, high_ref, above_ref, below_ref = rest[hosts + 10 : hosts + 14]
    wc_ref, wm_ref, wi_ref, wo_ref, weight_ref = rest[hosts + 14 : hosts + 19]
    load_sem, save_sem, fetch_sem, partial_sem = rest[hosts + 19 :]
    cells_x, cells_y, width = latent_ref.shape
    sources = (low_hbm, high_hbm, above_hbm, below_hbm, wc_hbm, wm_hbm, wi_hbm, wo_hbm, weight_hbm)
    targets = (low_ref, high_ref, above_ref, below_ref, wc_ref, wm_ref, wi_ref, wo_ref, weight_ref)
    fetches = [
        pltpu.make_async_copy(source, target, fetch_sem.at[number])
        for number, (source, target) in enumerate(zip(sources, targets))
    ]
    for fetch in fetches[:5]:
        fetch.start()
    me, strip = lax.axis_index("gy"), lax.axis_index("gx")
    flags = (me > 0, me < hosts - 1, strip > 0, strip < lax.axis_size("gx") - 1)
    chunks = cells_x // rows_per_chunk
    loaded = 8
    loads = cells_x // loaded

    def load(chunk):
        part = pl.ds(chunk * loaded, loaded)
        return pltpu.make_async_copy(latent_ref.at[part], cells_ref.at[part], load_sem.at[chunk])

    def save(chunk):
        part = pl.ds(chunk * rows_per_chunk, rows_per_chunk)
        return pltpu.make_async_copy(result_ref.at[part], refined_ref.at[part], save_sem.at[chunk])

    for chunk in range(loads):
        load(chunk).start()
    for fetch in fetches[5:]:
        fetch.start()
    lanes = 128
    size = partial_hbm[0].shape[0]
    total_ref[...] = jnp.zeros_like(total_ref)
    place = lax.broadcasted_iota(jnp.int32, (cells_y, width), 0)

    def project(cells):
        return dot(cells, wn_ref[...]).astype(BF16).astype(F32)

    def present(number, proj):
        return jnp.where(flags[number], proj, 0.0)

    def store_row(row, proj):
        low = side_ref[0, pl.ds(row, 1), :]
        high = side_ref[1, pl.ds(row, 1), :]
        proj_ref[1, row] = proj
        proj_ref[0, row] = jnp.where(place == 0, low, pltpu.roll(proj, 1, 0))
        proj_ref[2, row] = jnp.where(
            place == cells_y - 1, high, pltpu.roll(proj, cells_y - 1, 0)
        )

    for fetch in fetches[:5]:
        fetch.wait()
    side_ref[0, 1 : cells_x + 1, :] = present(0, project(low_ref[...]))
    side_ref[1, 1 : cells_x + 1, :] = present(1, project(high_ref[...]))
    for ref, number, row in ((above_ref, 2, 0), (below_ref, 3, cells_x + 1)):
        proj = present(number, project(ref[...]))
        for side in (0, 1):
            corner = proj[cells_y + side : cells_y + side + 1]
            side_ref[side, row : row + 1, :] = present(side, corner)
        store_row(row, proj[:cells_y])

    for d in range(8):
        count = None
        for slot in range(dir_ref.shape[0]):
            term = jnp.where(dir_ref[slot] == d, mask_ref[slot].astype(F32), 0.0)
            count = term if count is None else count + term
        count_ref[pl.ds(d, cells_x, stride=8), :] = count

    lowest = -embed_ref[...].astype(F32)
    shape = (8, 8 * lanes)
    own_lanes = lax.broadcasted_iota(jnp.int32, shape, 1) // lanes
    ones = (own_lanes == lax.broadcasted_iota(jnp.int32, shape, 0)).astype(BF16)

    def columns(x, rows):
        count = count_ref[pl.ds(pl.multiple_of(x * 8, 8), 8), :]
        return lax.dot_general(
            count.astype(BF16), rows, (((0,), (0,)), ((), ())), preferred_element_type=F32
        )

    def prepare(chunk, carry):
        first = chunk * loaded
        load(chunk).wait()
        cells = cells_ref[pl.ds(first, loaded)].reshape(-1, width)
        proj = project(cells)
        for row in range(loaded):
            store_row(first + row + 1, proj[row * cells_y : (row + 1) * cells_y])
            spread_ref[first + row] = columns(first + row, ones)
        center_ref[pl.ds(first, loaded)] = dot(cells, wc_ref[...]).reshape(loaded, cells_y, width)
        return carry

    lax.fori_loop(0, loads, prepare, 0)
    for fetch in fetches[5:]:
        fetch.wait()

    parts = [slice(half, half + lanes) for half in range(0, width, lanes)]

    def gather(row, inner):
        x = row
        for start in range(0, cells_y, 8):
            span = slice(start, start + 8)
            totals = [None] * len(parts)
            for d in range(8):
                count = spread_ref[row, span, d * lanes : (d + 1) * lanes]
                for number, part in enumerate(parts):
                    near = proj_ref[1 + STEP_Y[d], x + 1 + STEP_X[d], span, part]
                    hidden = jnp.maximum(
                        center_ref[row, span, part] + near, lowest[d : d + 1, part]
                    )
                    term = count * hidden
                    total = totals[number]
                    totals[number] = term if total is None else total + term
            for number, part in enumerate(parts):
                summed_ref[row, span, part] = totals[number]
        return inner

    lax.fori_loop(0, cells_x, gather, 0, unroll=2)

    def refine(chunk, carry):
        first = chunk * rows_per_chunk
        cells = cells_ref[pl.ds(first, rows_per_chunk)].reshape(-1, width)
        rest_sum = jnp.concatenate(
            [columns(first + row, embed_ref[...]) for row in range(rows_per_chunk)]
        )
        summed = summed_ref[pl.ds(first, rows_per_chunk)].reshape(-1, width)
        summed = (summed + rest_sum).astype(BF16)
        aggregate = dot(summed, wm_ref[...]).astype(BF16)
        hidden = dot(cells, wi_ref[:width]) + dot(aggregate, wi_ref[width:])
        hidden = jnp.maximum(hidden, 0.0).astype(BF16)
        refined = (cells.astype(F32) + dot(hidden, wo_ref[...])).astype(BF16)
        result_ref[pl.ds(first, rows_per_chunk)] = refined.reshape(
            rows_per_chunk, cells_y, width
        )
        save(chunk).start()
        for row in range(rows_per_chunk):
            x = first + row
            rows = weight_ref.shape[1]
            part = dot(weight_ref[x], refined[row * cells_y : (row + 1) * cells_y])
            cluster = (host_ref[x] ^ me) * (size // rows) + slot_ref[x]
            base = pl.multiple_of(cluster * rows, rows)
            total_ref[pl.ds(base, rows), :] += part
        return carry

    lax.fori_loop(0, chunks, refine, 0)
    outs = [
        pltpu.make_async_copy(partial_ref.at[host], partial_hbm[host], partial_sem.at[host])
        for host in range(hosts)
    ]
    for host in range(hosts):
        partial_ref[host] = total_ref[host * size : (host + 1) * size, :].astype(BF16)
        outs[host].start()
    for out in outs:
        out.wait()
    for chunk in range(chunks):
        save(chunk).wait()


def coarse_kernel(
    hosts,
    degree,
    host_ref,
    slot_ref,
    refined_ref,
    weight_ref,
    as_ref,
    ad_ref,
    am_ref,
    bi_ref,
    bo_ref,
    *rest,
):
    own_refs = rest[:hosts]
    next_refs = rest[hosts : 2 * hosts]
    out_ref, strip_ref, table_ref, rows_ref, dest_ref, summed_ref = rest[2 * hosts : 2 * hosts + 6]
    cells_ref, result_ref, raise_ref, index_ref, lined_ref, source_ref = rest[2 * hosts + 6 : -3]
    load_sem, save_sem, index_sem = rest[-3:]
    blocks, rows, _ = weight_ref.shape
    size, width = strip_ref.shape[0] // hosts, strip_ref.shape[1]
    lanes = 128
    me = lax.axis_index("gy")
    load = pltpu.make_async_copy(refined_ref, cells_ref, load_sem)
    load.start()

    def cluster_row(block):
        return ((host_ref[block] ^ me) * (size // rows) + slot_ref[block]) * rows

    half = width // 2
    for number, ref in enumerate(own_refs):
        digits = ref[size:, :].astype(F32).astype(jnp.int32)
        local = digits[:degree] * DIGIT + digits[degree : 2 * degree]
        local = 2 * (jnp.clip(local, 0, 2 * hosts * size - 1) ^ (me * size))
        for part in range(size // lanes):
            at = 8 * (number * (size // lanes) + part)
            index_ref[at : at + degree, :] = local[:, part * lanes : (part + 1) * lanes]

    group = lanes // rows
    owner = lax.broadcasted_iota(jnp.int32, (8, lanes), 1) // rows
    for start in range(0, blocks, group):
        lined = None
        for part in range(group):
            first = cluster_row(start + part)
            line = pl.multiple_of(8 * (first // lanes), 8)
            turned_by = (lanes + part * rows - first % lanes) % lanes
            moved = pltpu.roll(index_ref[pl.ds(line, 8), :], turned_by, 1)
            lined = moved if part == 0 else jnp.where(owner == part, moved, lined)
        at = 8 * (start // group)
        lined_ref[at : at + 8, :] = lined
    index_copy = pltpu.make_async_copy(lined_ref, source_ref, index_sem)
    index_copy.start()

    def split_store(ref, first, value):
        count = value.shape[0]
        ref[pl.ds(2 * first, count, stride=2), :] = value[:, :half]
        ref[pl.ds(2 * first + 1, count, stride=2), :] = value[:, half:]

    for number, ref in enumerate(own_refs + next_refs):
        proj = dot(ref[:size, :], as_ref[...]).astype(BF16).astype(F32)
        split_store(table_ref, number * size, proj)
    for number, ref in enumerate(own_refs):
        strip_ref[pl.ds(number * size, size), :] = ref[:size, :]

    def pick(block, carry):
        base = pl.multiple_of(cluster_row(block), rows)
        rows_ref[pl.ds(pl.multiple_of(block * rows, rows), rows), :] = strip_ref[
            pl.ds(base, rows), :
        ]
        return carry

    lax.fori_loop(0, blocks, pick, 0)
    for first in range(0, blocks * rows, 256):
        split_store(dest_ref, first, dot(rows_ref[first : first + 256, :], ad_ref[...]))

    index_copy.wait()

    def gather(number, carry):
        line = 8 * number
        for part in range(group):
            block = number * group + part
            raise_ref[block] = weight_ref[block].T
            for row in range(rows):
                at = pl.ds(pl.multiple_of(2 * (block * rows + row), 2), 2)
                dest = dest_ref[at, :]
                total = None
                for slot in range(degree):
                    source = source_ref[line + slot, part * rows + row]
                    near = table_ref[pl.ds(pl.multiple_of(source, 2), 2), :]
                    hidden = jnp.maximum(near + dest, 0.0)
                    total = hidden if total is None else total + hidden
                summed_ref[at, :] = total
        return carry

    lax.fori_loop(0, blocks // group, gather, 0)
    half_rows = blocks * rows // 2
    for first in (0, half_rows):
        base = rows_ref[first : first + half_rows, :]
        summed = jnp.concatenate(
            [summed_ref[pl.ds(2 * first + part, half_rows, stride=2), :] for part in (0, 1)],
            axis=1,
        ).astype(BF16)
        aggregate = dot(summed, am_ref[...]).astype(BF16)
        hidden = dot(base, bi_ref[:width]) + dot(aggregate, bi_ref[width:])
        hidden = jnp.maximum(hidden, 0.0).astype(BF16)
        rows_ref[first : first + half_rows, :] = (
            base.astype(F32) + dot(hidden, bo_ref[...])
        ).astype(BF16)
    step = 8
    load.wait()

    def save(number):
        part = pl.ds(number * step, step)
        return pltpu.make_async_copy(result_ref.at[part], out_ref.at[part], save_sem.at[number])

    def update(number, carry):
        for part in range(step):
            block = number * step + part
            at = pl.ds(pl.multiple_of(block * rows, rows), rows)
            raised = dot(raise_ref[block], rows_ref[at, :])
            result_ref[block] = (cells_ref[block].astype(F32) + raised).astype(BF16)
        save(number).start()
        return carry

    lax.fori_loop(0, blocks // step, update, 0)
    for number in range(blocks // step):
        save(number).wait()


def turned(value, axis, step):
    count = lax.axis_size(axis)
    return lax.ppermute(value, axis, [(i, (i + step) % count) for i in range(count)])


def swapped(value, axis, distance):
    count = lax.axis_size(axis)
    return lax.ppermute(value, axis, [(i, i ^ distance) for i in range(count)])


def per_device(
    fine_latent,
    nbr_dir,
    nbr_mask,
    dir_embed,
    w_center,
    w_neighbour,
    w_msg,
    w_node_in,
    w_node_out,
    restrict_weight,
    cluster_host,
    cluster_slot,
    coarse_src,
    a_src,
    a_dst,
    a_msg,
    b_in,
    b_out,
):
    cells_x, cells_y, width = fine_latent.shape
    hosts = lax.axis_size("gy")
    outer = 4
    inner = hosts // outer
    me = lax.axis_index("gy")
    weights = restrict_weight[0]
    blocks, rows, _ = weights.shape
    per_host = blocks // 4
    size = per_host * rows
    degree = coarse_src.shape[1]

    low = turned(fine_latent[:, -1, :], "gy", 1)
    high = turned(fine_latent[:, 0, :], "gy", -1)
    fill = jnp.zeros((14, width), BF16)
    above = turned(jnp.concatenate([fine_latent[-1], low[-1:], high[-1:], fill]), "gx", 1)
    below = turned(jnp.concatenate([fine_latent[0], low[:1], high[:1], fill]), "gx", -1)
    vmem = pl.BlockSpec(memory_space=pltpu.VMEM)
    smem = pl.BlockSpec(memory_space=pltpu.SMEM)
    hbm = pl.BlockSpec(memory_space=pl.ANY)
    block_host, block_slot = cluster_host[0, :, 0], cluster_slot[0]
    chunk = 16
    fetched = (low, high, above, below, w_center, w_msg, w_node_in, w_node_out, weights)
    fine = pl.pallas_call(
        functools.partial(fine_kernel, hosts, chunk),
        out_shape=[jax.ShapeDtypeStruct(fine_latent.shape, BF16)]
        + [jax.ShapeDtypeStruct((size, width), BF16)] * hosts,
        in_specs=[smem] * 2 + [hbm] * 10 + [vmem] * 4,
        out_specs=[hbm] * (1 + hosts),
        scratch_shapes=[
            pltpu.VMEM((3, cells_x + 2, cells_y, width), F32),
            pltpu.VMEM((cells_x, cells_y, width), F32),
            pltpu.VMEM((cells_x, cells_y, width), F32),
            pltpu.VMEM((2, cells_x + 8, width), F32),
            pltpu.VMEM((hosts * size, width), F32),
            pltpu.VMEM((cells_x * 8, cells_y), F32),
            pltpu.VMEM((cells_x, cells_y, 8 * 128), F32),
            pltpu.VMEM(fine_latent.shape, BF16),
            pltpu.VMEM(fine_latent.shape, BF16),
            pltpu.VMEM((hosts, size, width), BF16),
        ]
        + [pltpu.VMEM(value.shape, BF16) for value in fetched]
        + [
            pltpu.SemaphoreType.DMA((cells_x // 8,)),
            pltpu.SemaphoreType.DMA((cells_x // chunk,)),
            pltpu.SemaphoreType.DMA((len(fetched),)),
            pltpu.SemaphoreType.DMA((hosts,)),
        ],
        compiler_params=pltpu.CompilerParams(vmem_limit_bytes=VMEM_LIMIT),
        name="fine_cells",
    )(
        block_host,
        block_slot,
        fine_latent,
        *fetched,
        jnp.swapaxes(nbr_dir, 0, 1),
        jnp.swapaxes(nbr_mask, 0, 1),
        dir_embed,
        w_neighbour,
    )
    refined, partial = fine[0], fine[1:]

    parts = {}
    for far in reversed(range(outer)):
        total = partial[far * inner].astype(F32)
        for near in range(1, inner):
            total = total + swapped(partial[far * inner + near], "gy", near).astype(F32)
        parts[far] = total
    coarse_in = parts[0]
    for far in reversed(range(1, outer)):
        coarse_in = coarse_in + swapped(parts[far].astype(BF16), "gy", far * inner).astype(F32)
    strip_rows = hosts * size
    local = coarse_src.T - lax.axis_index("gx") * strip_rows
    digits = [(local // DIGIT).astype(BF16), (local % DIGIT).astype(BF16)]
    digits = jnp.concatenate(digits + [jnp.zeros((16 - 2 * degree, size), BF16)])
    coarse_in = jnp.concatenate([coarse_in.astype(BF16), digits])

    own = [None] * hosts
    own[0] = coarse_in
    far = outer // 2
    own[far * inner] = swapped(coarse_in, "gy", far * inner)
    for step in range(1, far):
        own[step * inner] = swapped(coarse_in, "gy", step * inner)
        own[(far + step) * inner] = swapped(own[far * inner], "gy", step * inner)
    for far in range(outer):
        for near in range(1, inner):
            own[far * inner + near] = swapped(own[far * inner], "gy", near)
    following = [turned(value, "gx", -1) for value in own]

    return pl.pallas_call(
        functools.partial(coarse_kernel, hosts, degree),
        out_shape=jax.ShapeDtypeStruct(fine_latent.shape, BF16),
        in_specs=[smem] * 2 + [hbm] + [vmem] * (6 + 2 * hosts),
        out_specs=hbm,
        scratch_shapes=[
            pltpu.VMEM((strip_rows, width), BF16),
            pltpu.VMEM((4 * strip_rows, width // 2), F32),
            pltpu.VMEM((blocks * rows, width), BF16),
            pltpu.VMEM((2 * blocks * rows, width // 2), F32),
            pltpu.VMEM((2 * blocks * rows, width // 2), F32),
            pltpu.VMEM(fine_latent.shape, BF16),
            pltpu.VMEM(fine_latent.shape, BF16),
            pltpu.VMEM((blocks, cells_y, rows), BF16),
            pltpu.VMEM((8 * strip_rows // 128, 128), jnp.int32),
            pltpu.VMEM((8 * blocks * rows // 128, 128), jnp.int32),
            pltpu.SMEM((8 * blocks * rows // 128, 128), jnp.int32),
            pltpu.SemaphoreType.DMA(()),
            pltpu.SemaphoreType.DMA((4,)),
            pltpu.SemaphoreType.DMA(()),
        ],
        compiler_params=pltpu.CompilerParams(vmem_limit_bytes=VMEM_LIMIT),
        name="coarse_rows",
    )(block_host, block_slot, refined, weights, a_src, a_dst, a_msg, b_in, b_out, *own, *following)


def solution(mesh):
    in_specs = (
        P("gx", "gy", None),
        P("gx", None, "gy"),
        P("gx", None, "gy"),
        P(),
        P(),
        P(),
        P(),
        P(),
        P(),
        P("gy", "gx", None, None),
        P("gy", "gx", None),
        P("gy", "gx"),
        P(("gx", "gy"), None),
        P(),
        P(),
        P(),
        P(),
        P(),
    )
    out_specs = P("gx", "gy", None)
    return jax.shard_map(
        per_device, mesh=mesh, in_specs=in_specs, out_specs=out_specs, check_vma=False
    )
```

```python
import functools

import jax
import jax.numpy as jnp
from jax import lax
from jax.experimental import pallas as pl
from jax.experimental.pallas import tpu as pltpu
from jax.sharding import PartitionSpec as P

STEP_X = (-1, -1, -1, 0, 0, 1, 1, 1)
STEP_Y = (-1, 0, 1, -1, 1, -1, 0, 1)
F32 = jnp.float32
BF16 = jnp.bfloat16
DIGIT = 128
VMEM_LIMIT = 56 << 20


def dot(a, b):
    return jnp.dot(a, b, preferred_element_type=F32)


def fine_kernel(
    hosts,
    rows_per_chunk,
    host_ref,
    slot_ref,
    latent_ref,
    low_hbm,
    high_hbm,
    above_hbm,
    below_hbm,
    wc_hbm,
    wm_hbm,
    wi_hbm,
    wo_hbm,
    weight_hbm,
    dir_ref,
    mask_ref,
    embed_ref,
    wn_ref,
    refined_ref,
    *rest,
):
    partial_hbm = rest[:hosts]
    proj_ref, center_ref, summed_ref, side_ref, total_ref, count_ref, spread_ref = rest[hosts : hosts + 7]
    cells_ref, result_ref, partial_ref = rest[hosts + 7 : hosts + 10]
    low_ref, high_ref, above_ref, below_ref = rest[hosts + 10 : hosts + 14]
    wc_ref, wm_ref, wi_ref, wo_ref, weight_ref = rest[hosts + 14 : hosts + 19]
    load_sem, save_sem, fetch_sem, partial_sem = rest[hosts + 19 :]
    cells_x, cells_y, width = latent_ref.shape
    sources = (low_hbm, high_hbm, above_hbm, below_hbm, wc_hbm, wm_hbm, wi_hbm, wo_hbm, weight_hbm)
    targets = (low_ref, high_ref, above_ref, below_ref, wc_ref, wm_ref, wi_ref, wo_ref, weight_ref)
    fetches = [
        pltpu.make_async_copy(source, target, fetch_sem.at[number])
        for number, (source, target) in enumerate(zip(sources, targets))
    ]
    for fetch in fetches[:5]:
        fetch.start()
    me, strip = lax.axis_index("gy"), lax.axis_index("gx")
    flags = (me > 0, me < hosts - 1, strip > 0, strip < lax.axis_size("gx") - 1)
    chunks = cells_x // rows_per_chunk
    loaded = 8
    loads = cells_x // loaded

    def load(chunk):
        part = pl.ds(chunk * loaded, loaded)
        return pltpu.make_async_copy(latent_ref.at[part], cells_ref.at[part], load_sem.at[chunk])

    def save(chunk):
        part = pl.ds(chunk * rows_per_chunk, rows_per_chunk)
        return pltpu.make_async_copy(result_ref.at[part], refined_ref.at[part], save_sem.at[chunk])

    for chunk in range(loads):
        load(chunk).start()
    for fetch in fetches[5:]:
        fetch.start()
    lanes = 128
    size = partial_hbm[0].shape[0]
    total_ref[...] = jnp.zeros_like(total_ref)
    place = lax.broadcasted_iota(jnp.int32, (cells_y, width), 0)

    def project(cells):
        return dot(cells, wn_ref[...]).astype(BF16).astype(F32)

    def present(number, proj):
        return jnp.where(flags[number], proj, 0.0)

    def store_row(row, proj):
        low = side_ref[0, pl.ds(row, 1), :]
        high = side_ref[1, pl.ds(row, 1), :]
        proj_ref[1, row] = proj
        proj_ref[0, row] = jnp.where(place == 0, low, pltpu.roll(proj, 1, 0))
        proj_ref[2, row] = jnp.where(
            place == cells_y - 1, high, pltpu.roll(proj, cells_y - 1, 0)
        )

    for fetch in fetches[:5]:
        fetch.wait()
    side_ref[0, 1 : cells_x + 1, :] = present(0, project(low_ref[...]))
    side_ref[1, 1 : cells_x + 1, :] = present(1, project(high_ref[...]))
    for ref, number, row in ((above_ref, 2, 0), (below_ref, 3, cells_x + 1)):
        proj = present(number, project(ref[...]))
        for side in (0, 1):
            corner = proj[cells_y + side : cells_y + side + 1]
            side_ref[side, row : row + 1, :] = present(side, corner)
        store_row(row, proj[:cells_y])

    for d in range(8):
        count = None
        for slot in range(dir_ref.shape[0]):
            term = jnp.where(dir_ref[slot] == d, mask_ref[slot].astype(F32), 0.0)
            count = term if count is None else count + term
        count_ref[pl.ds(d, cells_x, stride=8), :] = count

    lowest = -embed_ref[...].astype(F32)
    shape = (8, 8 * lanes)
    own_lanes = lax.broadcasted_iota(jnp.int32, shape, 1) // lanes
    ones = (own_lanes == lax.broadcasted_iota(jnp.int32, shape, 0)).astype(BF16)

    def columns(x, rows):
        count = count_ref[pl.ds(pl.multiple_of(x * 8, 8), 8), :]
        return lax.dot_general(
            count.astype(BF16), rows, (((0,), (0,)), ((), ())), preferred_element_type=F32
        )

    def prepare(chunk, carry):
        first = chunk * loaded
        load(chunk).wait()
        cells = cells_ref[pl.ds(first, loaded)].reshape(-1, width)
        proj = project(cells)
        for row in range(loaded):
            store_row(first + row + 1, proj[row * cells_y : (row + 1) * cells_y])
            spread_ref[first + row] = columns(first + row, ones)
        center_ref[pl.ds(first, loaded)] = dot(cells, wc_ref[...]).reshape(loaded, cells_y, width)
        return carry

    lax.fori_loop(0, loads, prepare, 0)
    for fetch in fetches[5:]:
        fetch.wait()

    parts = [slice(half, half + lanes) for half in range(0, width, lanes)]

    def gather(row, inner):
        x = row
        for start in range(0, cells_y, 8):
            span = slice(start, start + 8)
            totals = [None] * len(parts)
            for d in range(8):
                count = spread_ref[row, span, d * lanes : (d + 1) * lanes]
                for number, part in enumerate(parts):
                    near = proj_ref[1 + STEP_Y[d], x + 1 + STEP_X[d], span, part]
                    hidden = jnp.maximum(
                        center_ref[row, span, part] + near, lowest[d : d + 1, part]
                    )
                    term = count * hidden
                    total = totals[number]
                    totals[number] = term if total is None else total + term
            for number, part in enumerate(parts):
                summed_ref[row, span, part] = totals[number]
        return inner

    lax.fori_loop(0, cells_x, gather, 0, unroll=2)

    def refine(chunk, carry):
        first = chunk * rows_per_chunk
        cells = cells_ref[pl.ds(first, rows_per_chunk)].reshape(-1, width)
        rest_sum = jnp.concatenate(
            [columns(first + row, embed_ref[...]) for row in range(rows_per_chunk)]
        )
        summed = summed_ref[pl.ds(first, rows_per_chunk)].reshape(-1, width)
        summed = (summed + rest_sum).astype(BF16)
        aggregate = dot(summed, wm_ref[...]).astype(BF16)
        hidden = dot(cells, wi_ref[:width]) + dot(aggregate, wi_ref[width:])
        hidden = jnp.maximum(hidden, 0.0).astype(BF16)
        refined = (cells.astype(F32) + dot(hidden, wo_ref[...])).astype(BF16)
        result_ref[pl.ds(first, rows_per_chunk)] = refined.reshape(
            rows_per_chunk, cells_y, width
        )
        save(chunk).start()
        for row in range(rows_per_chunk):
            x = first + row
            rows = weight_ref.shape[1]
            part = dot(weight_ref[x], refined[row * cells_y : (row + 1) * cells_y])
            cluster = (host_ref[x] ^ me) * (size // rows) + slot_ref[x]
            base = pl.multiple_of(cluster * rows, rows)
            total_ref[pl.ds(base, rows), :] += part
        return carry

    lax.fori_loop(0, chunks, refine, 0)
    outs = [
        pltpu.make_async_copy(partial_ref.at[host], partial_hbm[host], partial_sem.at[host])
        for host in range(hosts)
    ]
    for host in range(hosts):
        partial_ref[host] = total_ref[host * size : (host + 1) * size, :].astype(BF16)
        outs[host].start()
    for out in outs:
        out.wait()
    for chunk in range(chunks):
        save(chunk).wait()


def coarse_kernel(
    hosts,
    degree,
    host_ref,
    slot_ref,
    refined_ref,
    weight_ref,
    as_ref,
    ad_ref,
    am_ref,
    bi_ref,
    bo_ref,
    *rest,
):
    own_refs = rest[:hosts]
    next_refs = rest[hosts : 2 * hosts]
    out_ref, strip_ref, table_ref, rows_ref, dest_ref, summed_ref = rest[2 * hosts : 2 * hosts + 6]
    cells_ref, result_ref, raise_ref, index_ref, lined_ref, source_ref = rest[2 * hosts + 6 : -3]
    load_sem, save_sem, index_sem = rest[-3:]
    blocks, rows, _ = weight_ref.shape
    size, width = strip_ref.shape[0] // hosts, strip_ref.shape[1]
    lanes = 128
    me = lax.axis_index("gy")
    load = pltpu.make_async_copy(refined_ref, cells_ref, load_sem)
    load.start()

    def cluster_row(block):
        return ((host_ref[block] ^ me) * (size // rows) + slot_ref[block]) * rows

    half = width // 2
    for number, ref in enumerate(own_refs):
        digits = ref[size:, :].astype(F32).astype(jnp.int32)
        local = digits[:degree] * DIGIT + digits[degree : 2 * degree]
        local = 2 * (jnp.clip(local, 0, 2 * hosts * size - 1) ^ (me * size))
        for part in range(size // lanes):
            at = 8 * (number * (size // lanes) + part)
            index_ref[at : at + degree, :] = local[:, part * lanes : (part + 1) * lanes]

    group = lanes // rows
    owner = lax.broadcasted_iota(jnp.int32, (8, lanes), 1) // rows
    for start in range(0, blocks, group):
        lined = None
        for part in range(group):
            first = cluster_row(start + part)
            line = pl.multiple_of(8 * (first // lanes), 8)
            turned_by = (lanes + part * rows - first % lanes) % lanes
            moved = pltpu.roll(index_ref[pl.ds(line, 8), :], turned_by, 1)
            lined = moved if part == 0 else jnp.where(owner == part, moved, lined)
        at = 8 * (start // group)
        lined_ref[at : at + 8, :] = lined
    index_copy = pltpu.make_async_copy(lined_ref, source_ref, index_sem)
    index_copy.start()

    def split_store(ref, first, value):
        count = value.shape[0]
        ref[pl.ds(2 * first, count, stride=2), :] = value[:, :half]
        ref[pl.ds(2 * first + 1, count, stride=2), :] = value[:, half:]

    for number, ref in enumerate(own_refs + next_refs):
        proj = dot(ref[:size, :], as_ref[...]).astype(BF16).astype(F32)
        split_store(table_ref, number * size, proj)
    for number, ref in enumerate(own_refs):
        strip_ref[pl.ds(number * size, size), :] = ref[:size, :]

    def pick(block, carry):
        base = pl.multiple_of(cluster_row(block), rows)
        rows_ref[pl.ds(pl.multiple_of(block * rows, rows), rows), :] = strip_ref[
            pl.ds(base, rows), :
        ]
        return carry

    lax.fori_loop(0, blocks, pick, 0)
    for first in range(0, blocks * rows, 256):
        split_store(dest_ref, first, dot(rows_ref[first : first + 256, :], ad_ref[...]))

    index_copy.wait()

    def gather(number, carry):
        line = 8 * number
        for part in range(group):
            block = number * group + part
            raise_ref[block] = weight_ref[block].T
            for row in range(rows):
                at = pl.ds(pl.multiple_of(2 * (block * rows + row), 2), 2)
                dest = dest_ref[at, :]
                total = None
                for slot in range(degree):
                    source = source_ref[line + slot, part * rows + row]
                    near = table_ref[pl.ds(pl.multiple_of(source, 2), 2), :]
                    hidden = jnp.maximum(near + dest, 0.0)
                    total = hidden if total is None else total + hidden
                summed_ref[at, :] = total
        return carry

    lax.fori_loop(0, blocks // group, gather, 0)
    half_rows = blocks * rows // 2
    for first in (0, half_rows):
        base = rows_ref[first : first + half_rows, :]
        summed = jnp.concatenate(
            [summed_ref[pl.ds(2 * first + part, half_rows, stride=2), :] for part in (0, 1)],
            axis=1,
        ).astype(BF16)
        aggregate = dot(summed, am_ref[...]).astype(BF16)
        hidden = dot(base, bi_ref[:width]) + dot(aggregate, bi_ref[width:])
        hidden = jnp.maximum(hidden, 0.0).astype(BF16)
        rows_ref[first : first + half_rows, :] = (
            base.astype(F32) + dot(hidden, bo_ref[...])
        ).astype(BF16)
    step = 8
    load.wait()

    def save(number):
        part = pl.ds(number * step, step)
        return pltpu.make_async_copy(result_ref.at[part], out_ref.at[part], save_sem.at[number])

    def update(number, carry):
        for part in range(step):
            block = number * step + part
            at = pl.ds(pl.multiple_of(block * rows, rows), rows)
            raised = dot(raise_ref[block], rows_ref[at, :])
            result_ref[block] = (cells_ref[block].astype(F32) + raised).astype(BF16)
        save(number).start()
        return carry

    lax.fori_loop(0, blocks // step, update, 0)
    for number in range(blocks // step):
        save(number).wait()


def turned(value, axis, step):
    count = lax.axis_size(axis)
    return lax.ppermute(value, axis, [(i, (i + step) % count) for i in range(count)])


def swapped(value, axis, distance):
    count = lax.axis_size(axis)
    return lax.ppermute(value, axis, [(i, i ^ distance) for i in range(count)])


def per_device(
    fine_latent,
    nbr_dir,
    nbr_mask,
    dir_embed,
    w_center,
    w_neighbour,
    w_msg,
    w_node_in,
    w_node_out,
    restrict_weight,
    cluster_host,
    cluster_slot,
    coarse_src,
    a_src,
    a_dst,
    a_msg,
    b_in,
    b_out,
):
    cells_x, cells_y, width = fine_latent.shape
    hosts = lax.axis_size("gy")
    outer = 4
    inner = hosts // outer
    me = lax.axis_index("gy")
    weights = restrict_weight[0]
    blocks, rows, _ = weights.shape
    per_host = blocks // 4
    size = per_host * rows
    degree = coarse_src.shape[1]

    low = turned(fine_latent[:, -1, :], "gy", 1)
    high = turned(fine_latent[:, 0, :], "gy", -1)
    fill = jnp.zeros((14, width), BF16)
    above = turned(jnp.concatenate([fine_latent[-1], low[-1:], high[-1:], fill]), "gx", 1)
    below = turned(jnp.concatenate([fine_latent[0], low[:1], high[:1], fill]), "gx", -1)
    vmem = pl.BlockSpec(memory_space=pltpu.VMEM)
    smem = pl.BlockSpec(memory_space=pltpu.SMEM)
    hbm = pl.BlockSpec(memory_space=pl.ANY)
    block_host, block_slot = cluster_host[0, :, 0], cluster_slot[0]
    chunk = 16
    fetched = (low, high, above, below, w_center, w_msg, w_node_in, w_node_out, weights)
    fine = pl.pallas_call(
        functools.partial(fine_kernel, hosts, chunk),
        out_shape=[jax.ShapeDtypeStruct(fine_latent.shape, BF16)]
        + [jax.ShapeDtypeStruct((size, width), BF16)] * hosts,
        in_specs=[smem] * 2 + [hbm] * 10 + [vmem] * 4,
        out_specs=[hbm] * (1 + hosts),
        scratch_shapes=[
            pltpu.VMEM((3, cells_x + 2, cells_y, width), F32),
            pltpu.VMEM((cells_x, cells_y, width), F32),
            pltpu.VMEM((cells_x, cells_y, width), F32),
            pltpu.VMEM((2, cells_x + 8, width), F32),
            pltpu.VMEM((hosts * size, width), F32),
            pltpu.VMEM((cells_x * 8, cells_y), F32),
            pltpu.VMEM((cells_x, cells_y, 8 * 128), F32),
            pltpu.VMEM(fine_latent.shape, BF16),
            pltpu.VMEM(fine_latent.shape, BF16),
            pltpu.VMEM((hosts, size, width), BF16),
        ]
        + [pltpu.VMEM(value.shape, BF16) for value in fetched]
        + [
            pltpu.SemaphoreType.DMA((cells_x // 8,)),
            pltpu.SemaphoreType.DMA((cells_x // chunk,)),
            pltpu.SemaphoreType.DMA((len(fetched),)),
            pltpu.SemaphoreType.DMA((hosts,)),
        ],
        compiler_params=pltpu.CompilerParams(vmem_limit_bytes=VMEM_LIMIT),
        name="fine_cells",
    )(
        block_host,
        block_slot,
        fine_latent,
        *fetched,
        jnp.swapaxes(nbr_dir, 0, 1),
        jnp.swapaxes(nbr_mask, 0, 1),
        dir_embed,
        w_neighbour,
    )
    refined, partial = fine[0], fine[1:]

    half = outer // 2
    parts = [value.astype(F32) for value in partial]

    def arrive(target, number, distance):
        parts[target] = parts[target] + swapped(partial[number], "gy", distance).astype(F32)

    for far in range(half + 1, outer):
        for near in range(1, inner):
            arrive(near, far * inner + near, far * inner)
        arrive(half * inner, far * inner, (far - half) * inner)
    for far in range(half, 0, -1):
        for near in range(1, inner):
            arrive(far * inner, far * inner + near, near)
    coarse_in = parts[0]
    for number in [far * inner for far in range(half, 0, -1)] + list(range(1, inner)):
        coarse_in = coarse_in + swapped(parts[number].astype(BF16), "gy", number).astype(F32)

    strip_rows = hosts * size
    local = coarse_src.T - lax.axis_index("gx") * strip_rows
    digits = [(local // DIGIT).astype(BF16), (local % DIGIT).astype(BF16)]
    digits = jnp.concatenate(digits + [jnp.zeros((16 - 2 * degree, size), BF16)])
    coarse_in = jnp.concatenate([coarse_in.astype(BF16), digits])

    own = [None] * hosts
    own[0] = coarse_in
    far = outer // 2
    own[far * inner] = swapped(coarse_in, "gy", far * inner)
    for step in range(1, far):
        own[step * inner] = swapped(coarse_in, "gy", step * inner)
        own[(far + step) * inner] = swapped(own[far * inner], "gy", step * inner)
    for far in range(outer):
        for near in range(1, inner):
            own[far * inner + near] = swapped(own[far * inner], "gy", near)
    following = [turned(value, "gx", -1) for value in own]

    return pl.pallas_call(
        functools.partial(coarse_kernel, hosts, degree),
        out_shape=jax.ShapeDtypeStruct(fine_latent.shape, BF16),
        in_specs=[smem] * 2 + [hbm] + [vmem] * (6 + 2 * hosts),
        out_specs=hbm,
        scratch_shapes=[
            pltpu.VMEM((strip_rows, width), BF16),
            pltpu.VMEM((4 * strip_rows, width // 2), F32),
            pltpu.VMEM((blocks * rows, width), BF16),
            pltpu.VMEM((2 * blocks * rows, width // 2), F32),
            pltpu.VMEM((2 * blocks * rows, width // 2), F32),
            pltpu.VMEM(fine_latent.shape, BF16),
            pltpu.VMEM(fine_latent.shape, BF16),
            pltpu.VMEM((blocks, cells_y, rows), BF16),
            pltpu.VMEM((8 * strip_rows // 128, 128), jnp.int32),
            pltpu.VMEM((8 * blocks * rows // 128, 128), jnp.int32),
            pltpu.SMEM((8 * blocks * rows // 128, 128), jnp.int32),
            pltpu.SemaphoreType.DMA(()),
            pltpu.SemaphoreType.DMA((4,)),
            pltpu.SemaphoreType.DMA(()),
        ],
        compiler_params=pltpu.CompilerParams(vmem_limit_bytes=VMEM_LIMIT),
        name="coarse_rows",
    )(block_host, block_slot, refined, weights, a_src, a_dst, a_msg, b_in, b_out, *own, *following)


def solution(mesh):
    in_specs = (
        P("gx", "gy", None),
        P("gx", None, "gy"),
        P("gx", None, "gy"),
        P(),
        P(),
        P(),
        P(),
        P(),
        P(),
        P("gy", "gx", None, None),
        P("gy", "gx", None),
        P("gy", "gx"),
        P(("gx", "gy"), None),
        P(),
        P(),
        P(),
        P(),
        P(),
    )
    out_specs = P("gx", "gy", None)
    return jax.shard_map(
        per_device, mesh=mesh, in_specs=in_specs, out_specs=out_specs, check_vma=False
    )
```

```python
import functools

import jax
import jax.numpy as jnp
from jax import lax
from jax.experimental import pallas as pl
from jax.experimental.pallas import tpu as pltpu
from jax.sharding import PartitionSpec as P

STEP_X = (-1, -1, -1, 0, 0, 1, 1, 1)
STEP_Y = (-1, 0, 1, -1, 1, -1, 0, 1)
F32 = jnp.float32
BF16 = jnp.bfloat16
DIGIT = 128
VMEM_LIMIT = 56 << 20


def dot(a, b):
    return jnp.dot(a, b, preferred_element_type=F32)


def fine_kernel(
    hosts,
    rows_per_chunk,
    host_ref,
    slot_ref,
    latent_ref,
    low_hbm,
    high_hbm,
    above_hbm,
    below_hbm,
    wc_hbm,
    wm_hbm,
    wi_hbm,
    wo_hbm,
    weight_hbm,
    dir_ref,
    mask_ref,
    embed_ref,
    wn_ref,
    refined_ref,
    *rest,
):
    partial_hbm = rest[:hosts]
    proj_ref, center_ref, summed_ref, side_ref, total_ref, count_ref, spread_ref = rest[hosts : hosts + 7]
    cells_ref, result_ref, partial_ref = rest[hosts + 7 : hosts + 10]
    low_ref, high_ref, above_ref, below_ref = rest[hosts + 10 : hosts + 14]
    wc_ref, wm_ref, wi_ref, wo_ref, weight_ref = rest[hosts + 14 : hosts + 19]
    load_sem, save_sem, fetch_sem, partial_sem = rest[hosts + 19 :]
    cells_x, cells_y, width = latent_ref.shape
    sources = (low_hbm, high_hbm, above_hbm, below_hbm, wc_hbm, wm_hbm, wi_hbm, wo_hbm, weight_hbm)
    targets = (low_ref, high_ref, above_ref, below_ref, wc_ref, wm_ref, wi_ref, wo_ref, weight_ref)
    fetches = [
        pltpu.make_async_copy(source, target, fetch_sem.at[number])
        for number, (source, target) in enumerate(zip(sources, targets))
    ]
    for fetch in fetches[:5]:
        fetch.start()
    me, strip = lax.axis_index("gy"), lax.axis_index("gx")
    flags = (me > 0, me < hosts - 1, strip > 0, strip < lax.axis_size("gx") - 1)
    chunks = cells_x // rows_per_chunk
    loaded = 8
    loads = cells_x // loaded

    def load(chunk):
        part = pl.ds(chunk * loaded, loaded)
        return pltpu.make_async_copy(latent_ref.at[part], cells_ref.at[part], load_sem.at[chunk])

    def save(chunk):
        part = pl.ds(chunk * rows_per_chunk, rows_per_chunk)
        return pltpu.make_async_copy(result_ref.at[part], refined_ref.at[part], save_sem.at[chunk])

    for chunk in range(loads):
        load(chunk).start()
    for fetch in fetches[5:]:
        fetch.start()
    lanes = 128
    size = partial_hbm[0].shape[0]
    total_ref[...] = jnp.zeros_like(total_ref)
    place = lax.broadcasted_iota(jnp.int32, (cells_y, width), 0)

    def project(cells):
        return dot(cells, wn_ref[...]).astype(BF16).astype(F32)

    def present(number, proj):
        return jnp.where(flags[number], proj, 0.0)

    def store_row(row, proj):
        low = side_ref[0, pl.ds(row, 1), :]
        high = side_ref[1, pl.ds(row, 1), :]
        proj_ref[1, row] = proj
        proj_ref[0, row] = jnp.where(place == 0, low, pltpu.roll(proj, 1, 0))
        proj_ref[2, row] = jnp.where(
            place == cells_y - 1, high, pltpu.roll(proj, cells_y - 1, 0)
        )

    for fetch in fetches[:5]:
        fetch.wait()
    side_ref[0, 1 : cells_x + 1, :] = present(0, project(low_ref[...]))
    side_ref[1, 1 : cells_x + 1, :] = present(1, project(high_ref[...]))
    for ref, number, row in ((above_ref, 2, 0), (below_ref, 3, cells_x + 1)):
        proj = present(number, project(ref[...]))
        for side in (0, 1):
            corner = proj[cells_y + side : cells_y + side + 1]
            side_ref[side, row : row + 1, :] = present(side, corner)
        store_row(row, proj[:cells_y])

    for d in range(8):
        count = None
        for slot in range(dir_ref.shape[0]):
            term = jnp.where(dir_ref[slot] == d, mask_ref[slot].astype(F32), 0.0)
            count = term if count is None else count + term
        count_ref[pl.ds(d, cells_x, stride=8), :] = count

    lowest = -embed_ref[...].astype(F32)
    shape = (8, 8 * lanes)
    own_lanes = lax.broadcasted_iota(jnp.int32, shape, 1) // lanes
    ones = (own_lanes == lax.broadcasted_iota(jnp.int32, shape, 0)).astype(BF16)

    def columns(x, rows):
        count = count_ref[pl.ds(pl.multiple_of(x * 8, 8), 8), :]
        return lax.dot_general(
            count.astype(BF16), rows, (((0,), (0,)), ((), ())), preferred_element_type=F32
        )

    def prepare(chunk, carry):
        first = chunk * loaded
        load(chunk).wait()
        cells = cells_ref[pl.ds(first, loaded)].reshape(-1, width)
        proj = project(cells)
        for row in range(loaded):
            store_row(first + row + 1, proj[row * cells_y : (row + 1) * cells_y])
            spread_ref[first + row] = columns(first + row, ones)
        center_ref[pl.ds(first, loaded)] = dot(cells, wc_ref[...]).reshape(loaded, cells_y, width)
        return carry

    lax.fori_loop(0, loads, prepare, 0)
    for fetch in fetches[5:]:
        fetch.wait()

    parts = [slice(half, half + lanes) for half in range(0, width, lanes)]

    def gather(row, inner):
        x = row
        for start in range(0, cells_y, 8):
            span = slice(start, start + 8)
            totals = [None] * len(parts)
            for d in range(8):
                count = spread_ref[row, span, d * lanes : (d + 1) * lanes]
                for number, part in enumerate(parts):
                    near = proj_ref[1 + STEP_Y[d], x + 1 + STEP_X[d], span, part]
                    hidden = jnp.maximum(
                        center_ref[row, span, part] + near, lowest[d : d + 1, part]
                    )
                    term = count * hidden
                    total = totals[number]
                    totals[number] = term if total is None else total + term
            for number, part in enumerate(parts):
                summed_ref[row, span, part] = totals[number]
        return inner

    lax.fori_loop(0, cells_x, gather, 0, unroll=2)

    def refine(chunk, carry):
        first = chunk * rows_per_chunk
        cells = cells_ref[pl.ds(first, rows_per_chunk)].reshape(-1, width)
        rest_sum = jnp.concatenate(
            [columns(first + row, embed_ref[...]) for row in range(rows_per_chunk)]
        )
        summed = summed_ref[pl.ds(first, rows_per_chunk)].reshape(-1, width)
        summed = (summed + rest_sum).astype(BF16)
        aggregate = dot(summed, wm_ref[...]).astype(BF16)
        hidden = dot(cells, wi_ref[:width]) + dot(aggregate, wi_ref[width:])
        hidden = jnp.maximum(hidden, 0.0).astype(BF16)
        refined = (cells.astype(F32) + dot(hidden, wo_ref[...])).astype(BF16)
        result_ref[pl.ds(first, rows_per_chunk)] = refined.reshape(
            rows_per_chunk, cells_y, width
        )
        save(chunk).start()
        for row in range(rows_per_chunk):
            x = first + row
            rows = weight_ref.shape[1]
            part = dot(weight_ref[x], refined[row * cells_y : (row + 1) * cells_y])
            cluster = (host_ref[x] ^ me) * (size // rows) + slot_ref[x]
            base = pl.multiple_of(cluster * rows, rows)
            total_ref[pl.ds(base, rows), :] += part
        return carry

    lax.fori_loop(0, chunks, refine, 0)
    outs = [
        pltpu.make_async_copy(partial_ref.at[host], partial_hbm[host], partial_sem.at[host])
        for host in range(hosts)
    ]
    for host in range(hosts):
        partial_ref[host] = total_ref[host * size : (host + 1) * size, :].astype(BF16)
        outs[host].start()
    for out in outs:
        out.wait()
    for chunk in range(chunks):
        save(chunk).wait()


def coarse_kernel(
    hosts,
    degree,
    host_ref,
    slot_ref,
    refined_ref,
    weight_ref,
    as_ref,
    ad_ref,
    am_ref,
    bi_ref,
    bo_ref,
    *rest,
):
    own_refs = rest[:hosts]
    next_refs = rest[hosts : 2 * hosts]
    out_ref, strip_ref, table_ref, rows_ref, dest_ref, summed_ref = rest[2 * hosts : 2 * hosts + 6]
    cells_ref, result_ref, raise_ref, index_ref, lined_ref, source_ref = rest[2 * hosts + 6 : -3]
    load_sem, save_sem, index_sem = rest[-3:]
    blocks, rows, _ = weight_ref.shape
    size, width = strip_ref.shape[0] // hosts, strip_ref.shape[1]
    lanes = 128
    me = lax.axis_index("gy")
    load = pltpu.make_async_copy(refined_ref, cells_ref, load_sem)
    load.start()

    def cluster_row(block):
        return ((host_ref[block] ^ me) * (size // rows) + slot_ref[block]) * rows

    half = width // 2
    for number, ref in enumerate(own_refs):
        digits = ref[size:, :].astype(F32).astype(jnp.int32)
        local = digits[:degree] * DIGIT + digits[degree : 2 * degree]
        local = 2 * (jnp.clip(local, 0, 2 * hosts * size - 1) ^ (me * size))
        for part in range(size // lanes):
            at = 8 * (number * (size // lanes) + part)
            index_ref[at : at + degree, :] = local[:, part * lanes : (part + 1) * lanes]

    group = lanes // rows
    owner = lax.broadcasted_iota(jnp.int32, (8, lanes), 1) // rows
    for start in range(0, blocks, group):
        lined = None
        for part in range(group):
            first = cluster_row(start + part)
            line = pl.multiple_of(8 * (first // lanes), 8)
            turned_by = (lanes + part * rows - first % lanes) % lanes
            moved = pltpu.roll(index_ref[pl.ds(line, 8), :], turned_by, 1)
            lined = moved if part == 0 else jnp.where(owner == part, moved, lined)
        at = 8 * (start // group)
        lined_ref[at : at + 8, :] = lined
    index_copy = pltpu.make_async_copy(lined_ref, source_ref, index_sem)
    index_copy.start()

    def split_store(ref, first, value):
        count = value.shape[0]
        ref[pl.ds(2 * first, count, stride=2), :] = value[:, :half]
        ref[pl.ds(2 * first + 1, count, stride=2), :] = value[:, half:]

    for number, ref in enumerate(own_refs + next_refs):
        proj = dot(ref[:size, :], as_ref[...]).astype(BF16).astype(F32)
        split_store(table_ref, number * size, proj)
    for number, ref in enumerate(own_refs):
        strip_ref[pl.ds(number * size, size), :] = ref[:size, :]

    def pick(block, carry):
        base = pl.multiple_of(cluster_row(block), rows)
        rows_ref[pl.ds(pl.multiple_of(block * rows, rows), rows), :] = strip_ref[
            pl.ds(base, rows), :
        ]
        return carry

    lax.fori_loop(0, blocks, pick, 0)
    for first in range(0, blocks * rows, 256):
        split_store(dest_ref, first, dot(rows_ref[first : first + 256, :], ad_ref[...]))

    index_copy.wait()

    def gather(number, carry):
        line = 8 * number
        for part in range(group):
            block = number * group + part
            raise_ref[block] = weight_ref[block].T
            for row in range(rows):
                at = pl.ds(pl.multiple_of(2 * (block * rows + row), 2), 2)
                dest = dest_ref[at, :]
                total = None
                for slot in range(degree):
                    source = source_ref[line + slot, part * rows + row]
                    near = table_ref[pl.ds(pl.multiple_of(source, 2), 2), :]
                    hidden = jnp.maximum(near + dest, 0.0)
                    total = hidden if total is None else total + hidden
                summed_ref[at, :] = total
        return carry

    lax.fori_loop(0, blocks // group, gather, 0)
    half_rows = blocks * rows // 2
    for first in (0, half_rows):
        base = rows_ref[first : first + half_rows, :]
        summed = jnp.concatenate(
            [summed_ref[pl.ds(2 * first + part, half_rows, stride=2), :] for part in (0, 1)],
            axis=1,
        ).astype(BF16)
        aggregate = dot(summed, am_ref[...]).astype(BF16)
        hidden = dot(base, bi_ref[:width]) + dot(aggregate, bi_ref[width:])
        hidden = jnp.maximum(hidden, 0.0).astype(BF16)
        rows_ref[first : first + half_rows, :] = (
            base.astype(F32) + dot(hidden, bo_ref[...])
        ).astype(BF16)
    step = 8
    load.wait()

    def save(number):
        part = pl.ds(number * step, step)
        return pltpu.make_async_copy(result_ref.at[part], out_ref.at[part], save_sem.at[number])

    def update(number, carry):
        for part in range(step):
            block = number * step + part
            at = pl.ds(pl.multiple_of(block * rows, rows), rows)
            raised = dot(raise_ref[block], rows_ref[at, :])
            result_ref[block] = (cells_ref[block].astype(F32) + raised).astype(BF16)
        save(number).start()
        return carry

    lax.fori_loop(0, blocks // step, update, 0)
    for number in range(blocks // step):
        save(number).wait()


def turned(value, axis, step):
    count = lax.axis_size(axis)
    return lax.ppermute(value, axis, [(i, (i + step) % count) for i in range(count)])


def swapped(value, axis, distance):
    count = lax.axis_size(axis)
    return lax.ppermute(value, axis, [(i, i ^ distance) for i in range(count)])


def per_device(
    fine_latent,
    nbr_dir,
    nbr_mask,
    dir_embed,
    w_center,
    w_neighbour,
    w_msg,
    w_node_in,
    w_node_out,
    restrict_weight,
    cluster_host,
    cluster_slot,
    coarse_src,
    a_src,
    a_dst,
    a_msg,
    b_in,
    b_out,
):
    cells_x, cells_y, width = fine_latent.shape
    hosts = lax.axis_size("gy")
    outer = 4
    inner = hosts // outer
    me = lax.axis_index("gy")
    weights = restrict_weight[0]
    blocks, rows, _ = weights.shape
    per_host = blocks // 4
    size = per_host * rows
    degree = coarse_src.shape[1]

    low = turned(fine_latent[:, -1, :], "gy", 1)
    high = turned(fine_latent[:, 0, :], "gy", -1)
    fill = jnp.zeros((14, width), BF16)
    above = turned(jnp.concatenate([fine_latent[-1], low[-1:], high[-1:], fill]), "gx", 1)
    below = turned(jnp.concatenate([fine_latent[0], low[:1], high[:1], fill]), "gx", -1)
    vmem = pl.BlockSpec(memory_space=pltpu.VMEM)
    smem = pl.BlockSpec(memory_space=pltpu.SMEM)
    hbm = pl.BlockSpec(memory_space=pl.ANY)
    block_host, block_slot = cluster_host[0, :, 0], cluster_slot[0]
    chunk = 16
    fetched = (low, high, above, below, w_center, w_msg, w_node_in, w_node_out, weights)
    fine = pl.pallas_call(
        functools.partial(fine_kernel, hosts, chunk),
        out_shape=[jax.ShapeDtypeStruct(fine_latent.shape, BF16)]
        + [jax.ShapeDtypeStruct((size, width), BF16)] * hosts,
        in_specs=[smem] * 2 + [hbm] * 10 + [vmem] * 4,
        out_specs=[hbm] * (1 + hosts),
        scratch_shapes=[
            pltpu.VMEM((3, cells_x + 2, cells_y, width), F32),
            pltpu.VMEM((cells_x, cells_y, width), F32),
            pltpu.VMEM((cells_x, cells_y, width), F32),
            pltpu.VMEM((2, cells_x + 8, width), F32),
            pltpu.VMEM((hosts * size, width), F32),
            pltpu.VMEM((cells_x * 8, cells_y), F32),
            pltpu.VMEM((cells_x, cells_y, 8 * 128), F32),
            pltpu.VMEM(fine_latent.shape, BF16),
            pltpu.VMEM(fine_latent.shape, BF16),
            pltpu.VMEM((hosts, size, width), BF16),
        ]
        + [pltpu.VMEM(value.shape, BF16) for value in fetched]
        + [
            pltpu.SemaphoreType.DMA((cells_x // 8,)),
            pltpu.SemaphoreType.DMA((cells_x // chunk,)),
            pltpu.SemaphoreType.DMA((len(fetched),)),
            pltpu.SemaphoreType.DMA((hosts,)),
        ],
        compiler_params=pltpu.CompilerParams(vmem_limit_bytes=VMEM_LIMIT),
        name="fine_cells",
    )(
        block_host,
        block_slot,
        fine_latent,
        *fetched,
        jnp.swapaxes(nbr_dir, 0, 1),
        jnp.swapaxes(nbr_mask, 0, 1),
        dir_embed,
        w_neighbour,
    )
    refined, partial = fine[0], fine[1:]

    half = outer // 2
    parts = [value.astype(F32) for value in partial]

    def arrive(target, number, distance):
        parts[target] = parts[target] + swapped(partial[number], "gy", distance).astype(F32)

    for far in range(half + 1, outer):
        for near in range(1, inner):
            arrive(near, far * inner + near, far * inner)
        arrive(half * inner, far * inner, (far - half) * inner)
    for far in range(half, 0, -1):
        for near in range(1, inner):
            arrive(far * inner, far * inner + near, near)
    coarse_in = parts[0]
    for number in [far * inner for far in range(half, 0, -1)] + list(range(1, inner)):
        coarse_in = coarse_in + swapped(parts[number].astype(BF16), "gy", number).astype(F32)

    strip_rows = hosts * size
    local = coarse_src.T - lax.axis_index("gx") * strip_rows
    digits = [(local // DIGIT).astype(BF16), (local % DIGIT).astype(BF16)]
    digits = jnp.concatenate(digits + [jnp.zeros((16 - 2 * degree, size), BF16)])
    coarse_in = jnp.concatenate([coarse_in.astype(BF16), digits])

    own = [None] * hosts
    own[0] = coarse_in
    far = outer // 2
    own[far * inner] = swapped(coarse_in, "gy", far * inner)
    for step in range(1, far):
        own[step * inner] = swapped(coarse_in, "gy", step * inner)
        own[(far + step) * inner] = swapped(own[far * inner], "gy", step * inner)
    for near in range(1, inner):
        own[near] = swapped(coarse_in, "gy", near)
    for far in range(1, outer):
        for near in range(1, inner):
            if far > outer // 2:
                own[far * inner + near] = swapped(own[near], "gy", far * inner)
            else:
                own[far * inner + near] = swapped(own[far * inner], "gy", near)
    following = [turned(value, "gx", -1) for value in own]

    return pl.pallas_call(
        functools.partial(coarse_kernel, hosts, degree),
        out_shape=jax.ShapeDtypeStruct(fine_latent.shape, BF16),
        in_specs=[smem] * 2 + [hbm] + [vmem] * (6 + 2 * hosts),
        out_specs=hbm,
        scratch_shapes=[
            pltpu.VMEM((strip_rows, width), BF16),
            pltpu.VMEM((4 * strip_rows, width // 2), F32),
            pltpu.VMEM((blocks * rows, width), BF16),
            pltpu.VMEM((2 * blocks * rows, width // 2), F32),
            pltpu.VMEM((2 * blocks * rows, width // 2), F32),
            pltpu.VMEM(fine_latent.shape, BF16),
            pltpu.VMEM(fine_latent.shape, BF16),
            pltpu.VMEM((blocks, cells_y, rows), BF16),
            pltpu.VMEM((8 * strip_rows // 128, 128), jnp.int32),
            pltpu.VMEM((8 * blocks * rows // 128, 128), jnp.int32),
            pltpu.SMEM((8 * blocks * rows // 128, 128), jnp.int32),
            pltpu.SemaphoreType.DMA(()),
            pltpu.SemaphoreType.DMA((4,)),
            pltpu.SemaphoreType.DMA(()),
        ],
        compiler_params=pltpu.CompilerParams(vmem_limit_bytes=VMEM_LIMIT),
        name="coarse_rows",
    )(block_host, block_slot, refined, weights, a_src, a_dst, a_msg, b_in, b_out, *own, *following)


def solution(mesh):
    in_specs = (
        P("gx", "gy", None),
        P("gx", None, "gy"),
        P("gx", None, "gy"),
        P(),
        P(),
        P(),
        P(),
        P(),
        P(),
        P("gy", "gx", None, None),
        P("gy", "gx", None),
        P("gy", "gx"),
        P(("gx", "gy"), None),
        P(),
        P(),
        P(),
        P(),
        P(),
    )
    out_specs = P("gx", "gy", None)
    return jax.shard_map(
        per_device, mesh=mesh, in_specs=in_specs, out_specs=out_specs, check_vma=False
    )
```
